256 devices in a mesh: dp: 8 (over y, x_lo), mp: 32 (over x_hi, z, core).
Axes of the slice: x: 4 (x_hi: 2, x_lo: 2; x = x_hi * 2 + x_lo), y: 4, z: 8, core: 2. Of those that a mesh axis runs over, the one named last changes fastest.
Arguments:
- block_input: bfloat16 [2048, 6144], P('mp', 'dp'), may hold values from -200 to 200
- ln_gain: float32 [6144], P('dp'), may hold values from 0.1 to 1.9
- qkv_act: bfloat16 [2048, 12288], P('dp', 'mp'), may hold values from -6 to 6
- mlp_pre: bfloat16 [2048, 24576], P('dp', 'mp'), may hold values from -6 to 6
- out_grad: bfloat16 [2048, 6144], P('mp', 'dp'), may hold values from -160 to 160
- w_qkv: bfloat16 [6144, 12288], P('dp', 'mp'), may hold values from -0.078125 to 0.078125
- w_mlp: bfloat16 [6144, 24576], P('dp', 'mp')
- w_out_attn: bfloat16 [4096, 6144], P('mp', 'dp'), may hold values from -0.03125 to 0.03125
- w_out_mlp: bfloat16 [24576, 6144], P('mp', 'dp'), may hold values from -0.03125 to 0.03125
Outputs:
- input_grad: bfloat16 [2048, 6144], P('mp', 'dp')
- grad_qkv: bfloat16 [6144, 12288], P('dp', 'mp')
- grad_mlp: bfloat16 [6144, 24576], P('dp', 'mp')
- grad_out_attn: bfloat16 [4096, 6144], P('mp', 'dp')
- grad_out_mlp: bfloat16 [24576, 6144], P('mp', 'dp')
- gain_grad: float32 [6144], P('dp')
The draws below stay inside these ranges and needn't reach their ends.
All inputs are finite; a program needn't handle non-finite values.
Results may differ from the reference program's by a relative error of at most 0.029.
Values may be sent and summed in bfloat16 or wider, within the bound.
No kernel may reach another device: no remote copies, remote signals or barrier semaphores. Data moves between devices by JAX's collectives and lax.ppermute only.
A program may use at most 128 MiB of HBM per device.

```python
import math
import jax
import jax.numpy as jnp
from jax import lax

D = 6144
HD = 128
PATCH = 256
HEADS = 32
FF = 24576
ATTN = 4096
TOKENS = 2048
N_DP = 8


def draw_block_input(key, part):
    key = jax.random.fold_in(key, 5)
    row_key, value_key = jax.random.split(key)
    position = jnp.arange(D, dtype=jnp.float32)[None, :] / D
    values = jax.random.truncated_normal(value_key, -5.0, 5.0, (TOKENS, D), jnp.float32) + 0.6
    row_scale = jnp.exp(jax.random.uniform(row_key, (TOKENS, 1), jnp.float32, 0.0, math.log(3.0)))
    return (values * row_scale * jnp.power(3.0, position)).astype(jnp.bfloat16)


def draw_out_grad(key, part):
    key = jax.random.fold_in(key, 7)
    value_key = jax.random.fold_in(key, 1)
    position = jnp.arange(TOKENS, dtype=jnp.float32)[:, None] / TOKENS
    values = jax.random.truncated_normal(value_key, -5.0, 5.0, (TOKENS, D), jnp.float32)
    return (values * jnp.power(3.0, position)).astype(jnp.bfloat16)


def draw_w_mlp(key, part):
    key = jax.random.fold_in(key, 13)
    noise_key, column_key = jax.random.split(key)
    noise = jax.random.truncated_normal(noise_key, -5.0, 5.0, (D, FF), jnp.float32) / math.sqrt(D)
    column_part = jax.random.truncated_normal(column_key, -4.0, 4.0, (1, FF), jnp.float32) * (2.0 / math.sqrt(FF))
    profile = jnp.power(3.0, jnp.arange(D, dtype=jnp.float32)[:, None] / D)
    return (noise + column_part * profile).astype(jnp.bfloat16)


def draw_qkv_act(key, part):
    key = jax.random.fold_in(key, 11)
    images = TOKENS // PATCH
    shape = (images, PATCH, HEADS, 3, HD)
    values = jax.random.truncated_normal(key, -4.0, 4.0, shape, jnp.float32)
    return values.reshape(TOKENS, 3 * HEADS * HD).astype(jnp.bfloat16)


def shard_levels(own_key, dims, cuts, smallest, largest):
    def one(dim, shards_of):
        heights = jax.random.uniform(jax.random.fold_in(jax.random.fold_in(own_key, 6), dim), (shards_of,), jnp.float32, smallest / len(cuts), largest / len(cuts))
        return jnp.repeat(jnp.exp(heights), dims[dim] // shards_of).reshape((-1,) + (1,) * (len(dims) - dim - 1))

    loudness = one(*cuts[0])
    for cut in cuts[1:]:
        loudness = loudness * one(*cut)
    return loudness


def normal_values(stream_key, extent, spread, most, cuts=(), kind=jnp.bfloat16):
    result = spread * jax.random.normal(stream_key, extent, jnp.float32)
    if cuts:
        result = result * shard_levels(stream_key, extent, cuts, -0.22, 0.18)
    return jnp.clip(result, -most, most).astype(kind)


def setup_inputs(seed: int = 0) -> dict:
    splits = jax.random.split(jax.random.key(seed), 10)
    block_input = draw_block_input(jax.random.fold_in(splits[9], 71), 0)
    ln_gain = jnp.clip(1.0 + 0.18 * jax.random.normal(splits[1], (D,), jnp.float32), 0.1, 1.9)
    qkv_act = draw_qkv_act(jax.random.fold_in(splits[9], 71), 0)
    mlp_pre = normal_values(splits[3], (TOKENS, FF), 1.0, 6.0, ((0, 8), (1, 32)))
    out_grad = draw_out_grad(jax.random.fold_in(splits[9], 71), 0)
    w_qkv = normal_values(splits[5], (D, 3 * ATTN), D ** -0.5, 0.078125, ((0, 8), (1, 32)))
    w_mlp = draw_w_mlp(jax.random.fold_in(splits[9], 71), 0)
    w_out_attn = normal_values(splits[7], (ATTN, D), (ATTN + FF) ** -0.5, 0.03125, ((0, 32), (1, 8)))
    w_out_mlp = normal_values(splits[8], (FF, D), (ATTN + FF) ** -0.5, 0.03125, ((0, 32), (1, 8)))
    return dict(block_input=block_input, ln_gain=ln_gain, qkv_act=qkv_act, mlp_pre=mlp_pre, out_grad=out_grad, w_qkv=w_qkv, w_mlp=w_mlp, w_out_attn=w_out_attn, w_out_mlp=w_out_mlp)


eps = 1e-06

def attend(qkv_rows):
    row_count, col_count = qkv_rows.shape
    head_count = col_count // (3 * HD)
    pieces = qkv_rows.astype(jnp.float32).reshape(row_count // PATCH, PATCH, head_count, 3, HD)
    factor = HD ** (-0.5)
    scores = jnp.einsum('bqhd,bkhd->bhqk', pieces[:, :, :, 0], pieces[:, :, :, 1]) * factor
    scores = scores - lax.optimization_barrier(jnp.max(scores, axis=-1, keepdims=True))
    powers = jnp.exp(scores)
    attn_probs = powers / lax.optimization_barrier(jnp.sum(powers, axis=-1, keepdims=True))
    rounded = attn_probs.astype(jnp.bfloat16).astype(jnp.float32)
    attended = jnp.einsum('bhqk,bkhd->bqhd', rounded, pieces[:, :, :, 2])
    return (attended.astype(jnp.bfloat16).reshape(row_count, head_count * HD), attn_probs)

def attend_back(qkv_rows, attn_probs, grad_rows):
    row_count, col_count = qkv_rows.shape
    head_count = col_count // (3 * HD)
    pieces = qkv_rows.astype(jnp.float32).reshape(row_count // PATCH, PATCH, head_count, 3, HD)
    upward = grad_rows.astype(jnp.float32).reshape(row_count // PATCH, PATCH, head_count, HD)
    factor = HD ** (-0.5)
    rounded = attn_probs.astype(jnp.bfloat16).astype(jnp.float32)
    grad_value = jnp.einsum('bhqk,bqhd->bkhd', rounded, upward).astype(jnp.bfloat16)
    grad_probs = jnp.einsum('bqhd,bkhd->bhqk', upward, pieces[:, :, :, 2])
    centred = grad_probs - lax.optimization_barrier(jnp.sum(grad_probs * attn_probs, axis=-1, keepdims=True))
    grad_scores = (attn_probs * centred * factor).astype(jnp.bfloat16).astype(jnp.float32)
    grad_query = jnp.einsum('bhqk,bkhd->bqhd', grad_scores, pieces[:, :, :, 1]).astype(jnp.bfloat16)
    grad_key = jnp.einsum('bhqk,bqhd->bkhd', grad_scores, pieces[:, :, :, 0]).astype(jnp.bfloat16)
    stacked = jnp.stack([grad_query, grad_key, grad_value], axis=3)
    return stacked.reshape(row_count, col_count)

def gelu_back(preact_rows, incoming):
    values, pullback = jax.vjp(lambda inner: jax.nn.gelu(inner, approximate=True), preact_rows.astype(jnp.float32))
    return pullback(incoming)[0]

def reference(block_input, ln_gain, qkv_act, mlp_pre, out_grad, w_qkv, w_mlp, w_out_attn, w_out_mlp):
    widened = block_input.astype(jnp.float32)
    row_mean = lax.optimization_barrier(jnp.mean(widened, axis=1))
    centred = widened - row_mean[:, None]
    variance = lax.optimization_barrier(jnp.mean(centred * centred, axis=1))
    inverse = lax.rsqrt(variance + eps)
    normed = centred * inverse[:, None]
    scaled = (normed * ln_gain[None, :]).astype(jnp.bfloat16)
    attended, attn_probs = attend(qkv_act)
    activated = jax.nn.gelu(mlp_pre.astype(jnp.float32), approximate=True).astype(jnp.bfloat16)
    block_width = D // N_DP
    grad_attn = jnp.zeros((TOKENS, ATTN), jnp.float32)
    grad_hidden = jnp.zeros((TOKENS, FF), jnp.float32)
    for block_index in range(N_DP):
        columns = slice(block_index * block_width, (block_index + 1) * block_width)
        segment = out_grad[:, columns]
        part_attn = jnp.dot(segment, w_out_attn[:, columns].T, preferred_element_type=jnp.float32)
        part_mlp = jnp.dot(segment, w_out_mlp[:, columns].T, preferred_element_type=jnp.float32)
        grad_attn = grad_attn + lax.optimization_barrier(part_attn.astype(jnp.bfloat16)).astype(jnp.float32)
        grad_hidden = grad_hidden + lax.optimization_barrier(part_mlp.astype(jnp.bfloat16)).astype(jnp.float32)
    grad_out_attn = jnp.dot(attended.T, out_grad, preferred_element_type=jnp.float32).astype(jnp.bfloat16)
    grad_out_mlp = jnp.dot(activated.T, out_grad, preferred_element_type=jnp.float32).astype(jnp.bfloat16)
    grad_qkv_rows = attend_back(qkv_act, attn_probs, grad_attn.astype(jnp.bfloat16))
    grad_pre_rows = gelu_back(mlp_pre, grad_hidden).astype(jnp.bfloat16)
    grad_qkv = jnp.dot(scaled.T, grad_qkv_rows, preferred_element_type=jnp.float32).astype(jnp.bfloat16)
    grad_mlp = jnp.dot(scaled.T, grad_pre_rows, preferred_element_type=jnp.float32).astype(jnp.bfloat16)
    grad_normed = jnp.dot(grad_qkv_rows, w_qkv.T, preferred_element_type=jnp.float32)
    grad_normed = grad_normed + jnp.dot(grad_pre_rows, w_mlp.T, preferred_element_type=jnp.float32)
    weighted = grad_normed * ln_gain[None, :]
    mean_grad = lax.optimization_barrier(jnp.mean(weighted, axis=1))
    mean_cross = lax.optimization_barrier(jnp.mean(weighted * normed, axis=1))
    input_grad = out_grad.astype(jnp.float32) + inverse[:, None] * (weighted - mean_grad[:, None] - normed * mean_cross[:, None])
    gain_grad = lax.optimization_barrier(jnp.sum(grad_normed * normed, axis=0))
    return (input_grad.astype(jnp.bfloat16), grad_qkv, grad_mlp, grad_out_attn, grad_out_mlp, gain_grad)
```

```python
import functools
import jax
import jax.numpy as jnp
from jax import lax
from jax.experimental import pallas as pl
from jax.experimental.pallas import tpu as pltpu
from jax.sharding import PartitionSpec as P

D = 6144
HD = 128
PATCH = 256
eps = 1e-06
BF = jnp.bfloat16
F32 = jnp.float32

NY, NX, NH, NZ, NC = 4, 2, 2, 8, 2
ROWS = 64


def dp_perm(move):
    pairs = []
    for y in range(NY):
        for x in range(NX):
            to_y, to_x = move(y, x)
            pairs.append((y * NX + x, (to_y % NY) * NX + to_x))
    return pairs


def mp_perm(move):
    pairs = []
    for h in range(NH):
        for z in range(NZ):
            for c in range(NC):
                to_h, to_z, to_c = move(h, z, c)
                pairs.append(((h * NZ + z) * NC + c, (to_h * NZ + to_z % NZ) * NC + to_c))
    return pairs


X_SWAP = dp_perm(lambda y, x: (y, 1 - x))
Y_UP = dp_perm(lambda y, x: (y + 1, x))
Y_DOWN = dp_perm(lambda y, x: (y - 1, x))
Y_ONE = dp_perm(lambda y, x: (y ^ 1, x))
Y_TWO = dp_perm(lambda y, x: (y ^ 2, x))
H_SWAP = mp_perm(lambda h, z, c: (1 - h, z, c))
C_SWAP = mp_perm(lambda h, z, c: (h, z, 1 - c))
Z_UP = mp_perm(lambda h, z, c: (h, z + 1, c))
Z_DOWN = mp_perm(lambda h, z, c: (h, z - 1, c))
Z_XOR = [mp_perm(functools.partial(lambda bit, h, z, c: (h, z ^ bit, c), bit)) for bit in (1, 2, 4)]

OFFSETS = [(0, 0), (1, 0), (3, 0), (2, 0), (0, 1), (1, 1), (3, 1), (2, 1)]


def dp_send(array, perm):
    return lax.ppermute(array, "dp", perm)


def mp_send(array, perm):
    return lax.ppermute(array, "mp", perm)


def dp_place():
    index = lax.axis_index("dp")
    return index // NX, index % NX


def mp_place():
    index = lax.axis_index("mp")
    return index // (NZ * NC), (index // NC) % NZ, index % NC


def image_of(offset):
    y, x = dp_place()
    dy, dx = offset
    return ((y + dy) % NY) * NX + (x + dx) % NX


def dot(a, b, ca, cb):
    return lax.dot_general(a, b, (((ca,), (cb,)), ((), ())), preferred_element_type=F32)


def call(kernel, out_shape, n_in, in_any=(), scratch=(), flops=0, nbytes=0, limit=50):
    specs = [
        pl.BlockSpec(memory_space=pl.ANY if i in in_any else pltpu.VMEM) for i in range(n_in)
    ]
    outs = jax.tree.map(lambda _: pl.BlockSpec(memory_space=pltpu.VMEM), out_shape)
    return pl.pallas_call(
        kernel,
        out_shape=out_shape,
        in_specs=specs,
        out_specs=outs,
        scratch_shapes=list(scratch),
        compiler_params=pltpu.CompilerParams(vmem_limit_bytes=limit * 1024 * 1024),
        cost_estimate=pl.CostEstimate(flops=flops, bytes_accessed=nbytes, transcendentals=0),
    )


GELU_C = 0.7978845608028654
GELU_A = 0.044715


def attn_probs_of(query, key):
    scores = dot(query, key, 1, 1) * (HD**-0.5)
    scores = scores - jnp.max(scores, axis=-1, keepdims=True)
    powers = jnp.exp(scores)
    return powers / jnp.sum(powers, axis=-1, keepdims=True)


def forward_kernel(qkv_ref, pre_ref, act_ref):
    probs = attn_probs_of(qkv_ref[:, 0:HD], qkv_ref[:, HD : 2 * HD])
    attended = dot(probs.astype(BF), qkv_ref[:, 2 * HD : 3 * HD], 1, 0)
    act_ref[:, 0:HD] = attended.astype(BF)
    pre = pre_ref[...].astype(F32)
    inner = jnp.tanh(GELU_C * (pre + GELU_A * pre * pre * pre))
    act_ref[:, HD:] = (0.5 * pre * (1.0 + inner)).astype(BF)


def spread_kernel(own_ref, other_ref, w_attn_ref, w_mlp_ref, all_ref, *rest):
    parts, sem = rest[:8], rest[8]
    h, z, c = mp_place()
    copies = []
    for dz in range(NZ):
        for dh in range(NH):
            for dc in range(NC):
                spot = ((h + dh) % NH * NZ + (z + dz) % NZ) * NC + (c + dc) % NC
                source = (own_ref, other_ref)[dc]
                copies.append(
                    pltpu.make_async_copy(
                        source.at[dz, dh],
                        all_ref.at[pl.ds(pl.multiple_of(spot * ROWS, ROWS), ROWS)],
                        sem.at[dz, dh, dc],
                    )
                )
    for copy in copies:
        copy.start()
    for copy in copies:
        copy.wait()
    for offset, part in zip(OFFSETS, parts):
        start = pl.multiple_of(image_of(offset) * PATCH, PATCH)
        rows = all_ref[pl.ds(start, PATCH), :]
        part[:, 0:HD] = dot(rows, w_attn_ref[...], 1, 1).astype(BF)
        part[:, HD:] = dot(rows, w_mlp_ref[...], 1, 1).astype(BF)


def middle_kernel(qkv_ref, pre_ref, a_ref, b_ref, c_ref, d_ref, grad_ref):
    total = (
        a_ref[...].astype(F32)
        + b_ref[...].astype(F32)
        + c_ref[...].astype(F32)
        + d_ref[...].astype(F32)
    )
    upward = total[:, 0:HD].astype(BF)
    query, key, value = (qkv_ref[:, i * HD : (i + 1) * HD] for i in range(3))
    probs = attn_probs_of(query, key)
    rounded = probs.astype(BF)
    grad_value = dot(rounded, upward, 0, 0)
    grad_probs = dot(upward, value, 1, 1)
    centred = grad_probs - jnp.sum(grad_probs * probs, axis=-1, keepdims=True)
    grad_scores = (probs * centred * (HD**-0.5)).astype(BF)
    grad_ref[:, 0:HD] = dot(grad_scores, key, 1, 0).astype(BF)
    grad_ref[:, HD : 2 * HD] = dot(grad_scores, query, 0, 0).astype(BF)
    grad_ref[:, 2 * HD : 3 * HD] = grad_value.astype(BF)
    pre = pre_ref[...].astype(F32)
    inner = jnp.tanh(GELU_C * (pre + GELU_A * pre * pre * pre))
    slope = 0.5 * (1.0 + inner) + 0.5 * pre * (1.0 - inner * inner) * (
        GELU_C * (1.0 + 3.0 * GELU_A * pre * pre)
    )
    grad_ref[:, 3 * HD :] = (total[:, HD:] * slope).astype(BF)


def normed_kernel(*refs):
    grads, (w_qkv_ref, w_mlp_ref, mine_ref, other_ref) = refs[:8], refs[8:]
    h, z, c = mp_place()
    for offset, grad in zip(OFFSETS, grads):
        image = image_of(offset)
        rows = dot(grad[:, 0 : 3 * HD], w_qkv_ref[...], 1, 1) + dot(
            grad[:, 3 * HD :], w_mlp_ref[...], 1, 1
        )
        dh = (image // 4 + h) % NH
        for k in range(2):
            dz = ((image % 4) * 2 + k - z + NZ) % NZ
            first = rows[k * 128 : k * 128 + ROWS].astype(BF)
            second = rows[k * 128 + ROWS : (k + 1) * 128].astype(BF)
            mine_ref[dz, dh] = jnp.where(c == 0, first, second)
            other_ref[dz, dh] = jnp.where(c == 0, second, first)


def out_weights_kernel(*refs):
    acts, (all_ref, attn_ref, mlp_ref, acc_ref) = refs[:8], refs[8:]
    for k, (offset, act) in enumerate(zip(OFFSETS, acts)):
        start = pl.multiple_of(image_of(offset) * PATCH, PATCH)
        term = dot(act[...], all_ref[pl.ds(start, PATCH), :], 0, 0)
        if k == 0:
            acc_ref[...] = term
        else:
            acc_ref[...] += term
    attn_ref[...] = acc_ref[0:HD].astype(BF)
    mlp_ref[...] = acc_ref[HD:].astype(BF)


def in_weights_kernel(*refs):
    grads, (all_ref, w_qkv_ref, w_mlp_ref, qkv_ref, mlp_ref, gain_ref, acc_ref) = (
        refs[:8],
        refs[8:],
    )
    for k, (offset, grad) in enumerate(zip(OFFSETS, grads)):
        start = pl.multiple_of(image_of(offset) * PATCH, PATCH)
        term = dot(all_ref[pl.ds(start, PATCH), :], grad[...], 0, 0)
        if k == 0:
            acc_ref[...] = term
        else:
            acc_ref[...] += term
    qkv = acc_ref[:, 0 : 3 * HD]
    mlp = acc_ref[:, 3 * HD :]
    qkv_ref[...] = qkv.astype(BF)
    mlp_ref[...] = mlp.astype(BF)
    gain_ref[...] = jnp.sum(qkv * w_qkv_ref[...].astype(F32), axis=1, keepdims=True) + jnp.sum(
        mlp * w_mlp_ref[...].astype(F32), axis=1, keepdims=True
    )


def add(*terms):
    total = terms[0].astype(F32)
    for term in terms[1:]:
        total = total + term.astype(F32)
    return total.astype(BF)


def gather_dp(own):
    below = dp_send(own, Y_UP)
    above = dp_send(own, Y_DOWN)
    beside = dp_send(own, X_SWAP)
    beside_below = dp_send(beside, Y_UP)
    beside_above = dp_send(beside, Y_DOWN)
    far = dp_send(below, Y_UP)
    beside_far = dp_send(beside_above, Y_DOWN)
    return [own, above, below, far, beside, beside_above, beside_below, beside_far]


def scatter_dp(parts):
    own, above, below, far, beside, beside_above, beside_below, beside_far = parts
    down = dp_send(far, Y_DOWN)
    up = dp_send(beside_far, Y_UP)
    down_beside = dp_send(beside_below, Y_DOWN)
    up_beside = dp_send(add(beside_above, up), Y_UP)
    down_last = dp_send(add(below, down), Y_DOWN)
    up_last = dp_send(above, Y_UP)
    across = dp_send(add(beside, down_beside, up_beside), X_SWAP)
    return own, down_last, up_last, across


def gather_mp(own):
    pair = jnp.stack([own, mp_send(own, H_SWAP)])
    ups, downs = [pair], [pair]
    for _ in range(3):
        ups.append(mp_send(ups[-1], Z_UP))
        downs.append(mp_send(downs[-1], Z_DOWN))
    far = jnp.stack([mp_send(ups[3][0], Z_UP), mp_send(downs[3][1], Z_DOWN)])
    mine = jnp.stack([pair, downs[1], downs[2], downs[3], far, ups[3], ups[2], ups[1]])
    return mine, mp_send(mine, C_SWAP)


def scatter_mp(mine, other):
    received = mp_send(other, C_SWAP)
    held = add(mine, received)
    up = mp_send(held[4, 0], Z_UP)
    down = mp_send(held[4, 1], Z_DOWN)
    up = jnp.stack([add(held[3, 0], up), held[3, 1]])
    down = jnp.stack([held[5, 0], add(held[5, 1], down)])
    for step in (1, 2):
        up = mp_send(up, Z_UP)
        down = mp_send(down, Z_DOWN)
        up = add(held[3 - step], up)
        down = add(held[5 + step], down)
    up = mp_send(up, Z_UP)
    down = mp_send(down, Z_DOWN)
    across = mp_send(add(held[0, 1], up[1], down[1]), H_SWAP)
    return held[0, 0].astype(F32) + up[0].astype(F32) + down[0].astype(F32) + across.astype(F32)


def sum_dp(values):
    for perm in (X_SWAP, Y_ONE, Y_TWO):
        values = values + dp_send(values, perm)
    return values


def per_device(
    block_input, ln_gain, qkv_act, mlp_pre, out_grad, w_qkv, w_mlp, w_out_attn, w_out_mlp
):
    width = block_input.shape[1]
    shape = jax.ShapeDtypeStruct
    widened = block_input.astype(F32)
    mean = jnp.mean(widened, axis=1)
    square = jnp.sum(jnp.square(widened - mean[:, None]), axis=1)
    count = width
    for perm in (X_SWAP, Y_ONE, Y_TWO):
        theirs = dp_send(jnp.stack([mean, square]), perm)
        gap = mean - theirs[0]
        square = square + theirs[1] + gap * gap * (count / 2)
        mean = (mean + theirs[0]) * 0.5
        count = count * 2
    inverse = lax.rsqrt(square / D + eps)
    normed = (widened - mean[:, None]) * inverse[:, None]
    scaled = (normed * ln_gain[None, :]).astype(BF)
    all_scaled = lax.all_gather(scaled, "mp", axis=0, tiled=True)

    act = call(
        forward_kernel, shape((PATCH, 896), BF), 2, flops=10**8, nbytes=2 * 10**6
    )(qkv_act, mlp_pre)
    all_acts = gather_dp(act)
    mine, other = gather_mp(out_grad)
    all_grad, *parts = call(
        spread_kernel,
        [shape((2048, 768), BF)] + [shape((PATCH, 896), BF)] * 8,
        4,
        in_any=(0, 1),
        scratch=[pltpu.SemaphoreType.DMA((NZ, NH, NC))],
        flops=2 * 2048 * 768 * 896,
        nbytes=12 * 10**6,
    )(mine, other, w_out_attn, w_out_mlp)
    sums = scatter_dp(parts)
    grad = call(
        middle_kernel, shape((PATCH, 1152), BF), 6, flops=2 * 10**8, nbytes=3 * 10**6
    )(qkv_act, mlp_pre, *sums)
    grads = gather_dp(grad)
    mine, other = call(
        normed_kernel,
        [shape((NZ, NH, ROWS, 768), BF)] * 2,
        10,
        flops=2 * 2048 * 768 * 1152,
        nbytes=10 * 10**6,
    )(*grads, w_qkv, w_mlp)
    grad_normed = scatter_mp(mine, other)
    acc_attn, acc_mlp = call(
        out_weights_kernel,
        [shape((HD, 768), BF), shape((768, 768), BF)],
        9,
        scratch=[pltpu.VMEM((896, 768), F32)],
        flops=2 * 2048 * 768 * 896,
        nbytes=8 * 10**6,
    )(*all_acts, all_grad)
    acc_qkv, acc_pre, gain_part = call(
        in_weights_kernel,
        [shape((768, 384), BF), shape((768, 768), BF), shape((768, 1), F32)],
        11,
        scratch=[pltpu.VMEM((768, 1152), F32)],
        flops=2 * 2048 * 768 * 1152,
        nbytes=11 * 10**6,
    )(*grads, all_scaled, w_qkv, w_mlp)
    gain_grad = gain_part[:, 0] / ln_gain
    for perm in (C_SWAP, H_SWAP, *Z_XOR):
        gain_grad = gain_grad + mp_send(gain_grad, perm)
    weighted = grad_normed * ln_gain[None, :]
    sums = sum_dp(jnp.stack([jnp.sum(weighted, axis=1), jnp.sum(weighted * normed, axis=1)])) / D
    input_grad = out_grad.astype(F32) + inverse[:, None] * (
        weighted - sums[0][:, None] - normed * sums[1][:, None]
    )
    return (input_grad.astype(BF), acc_qkv, acc_pre, acc_attn, acc_mlp, gain_grad)


def solution(mesh):
    return jax.shard_map(
        per_device,
        mesh=mesh,
        in_specs=(
            P("mp", "dp"),
            P("dp"),
            P("dp", "mp"),
            P("dp", "mp"),
            P("mp", "dp"),
            P("dp", "mp"),
            P("dp", "mp"),
            P("mp", "dp"),
            P("mp", "dp"),
        ),
        out_specs=(
            P("mp", "dp"),
            P("dp", "mp"),
            P("dp", "mp"),
            P("mp", "dp"),
            P("mp", "dp"),
            P("dp"),
        ),
        check_vma=False,
    )
```

```python
import functools
import jax
import jax.numpy as jnp
from jax import lax
from jax.experimental import pallas as pl
from jax.experimental.pallas import tpu as pltpu
from jax.sharding import PartitionSpec as P

D = 6144
HD = 128
PATCH = 256
eps = 1e-06
BF = jnp.bfloat16
F32 = jnp.float32

NY, NX, NH, NZ, NC = 4, 2, 2, 8, 2
ROWS = 64


def dp_perm(move):
    pairs = []
    for y in range(NY):
        for x in range(NX):
            to_y, to_x = move(y, x)
            pairs.append((y * NX + x, (to_y % NY) * NX + to_x))
    return pairs


def mp_perm(move):
    pairs = []
    for h in range(NH):
        for z in range(NZ):
            for c in range(NC):
                to_h, to_z, to_c = move(h, z, c)
                pairs.append(((h * NZ + z) * NC + c, (to_h * NZ + to_z % NZ) * NC + to_c))
    return pairs


X_SWAP = dp_perm(lambda y, x: (y, 1 - x))
Y_UP = dp_perm(lambda y, x: (y + 1, x))
Y_DOWN = dp_perm(lambda y, x: (y - 1, x))
Y_ONE = dp_perm(lambda y, x: (y ^ 1, x))
Y_TWO = dp_perm(lambda y, x: (y ^ 2, x))
H_SWAP = mp_perm(lambda h, z, c: (1 - h, z, c))
C_SWAP = mp_perm(lambda h, z, c: (h, z, 1 - c))
Z_RING = mp_perm(lambda h, z, c: (h, z + 1 - 2 * c, c))
Z_XOR = [mp_perm(functools.partial(lambda bit, h, z, c: (h, z ^ bit, c), bit)) for bit in (1, 2, 4)]

OFFSETS = [(0, 0), (1, 0), (3, 0), (0, 1), (2, 0), (1, 1), (3, 1), (2, 1)]


def dp_send(array, perm):
    return lax.ppermute(array, "dp", perm)


def mp_send(array, perm):
    return lax.ppermute(array, "mp", perm)


def dp_place():
    index = lax.axis_index("dp")
    return index // NX, index % NX


def mp_place():
    index = lax.axis_index("mp")
    return index // (NZ * NC), (index // NC) % NZ, index % NC


def image_of(offset):
    y, x = dp_place()
    dy, dx = offset
    return ((y + dy) % NY) * NX + (x + dx) % NX


def dot(a, b, ca, cb):
    return lax.dot_general(a, b, (((ca,), (cb,)), ((), ())), preferred_element_type=F32)


def call(kernel, out_shape, n_in, in_any=(), scratch=(), flops=0, nbytes=0, limit=50):
    specs = [
        pl.BlockSpec(memory_space=pl.ANY if i in in_any else pltpu.VMEM) for i in range(n_in)
    ]
    outs = jax.tree.map(lambda _: pl.BlockSpec(memory_space=pltpu.VMEM), out_shape)
    return pl.pallas_call(
        kernel,
        out_shape=out_shape,
        in_specs=specs,
        out_specs=outs,
        scratch_shapes=list(scratch),
        compiler_params=pltpu.CompilerParams(vmem_limit_bytes=limit * 1024 * 1024),
        cost_estimate=pl.CostEstimate(flops=flops, bytes_accessed=nbytes, transcendentals=0),
    )


GELU_C = 0.7978845608028654
GELU_A = 0.044715


def attn_probs_of(query, key):
    scores = dot(query, key, 1, 1) * (HD**-0.5)
    scores = scores - jnp.max(scores, axis=-1, keepdims=True)
    powers = jnp.exp(scores)
    return powers / jnp.sum(powers, axis=-1, keepdims=True)


def forward_kernel(qkv_ref, pre_ref, act_ref):
    probs = attn_probs_of(qkv_ref[:, 0:HD], qkv_ref[:, HD : 2 * HD])
    attended = dot(probs.astype(BF), qkv_ref[:, 2 * HD : 3 * HD], 1, 0)
    act_ref[:, 0:HD] = attended.astype(BF)
    pre = pre_ref[...].astype(F32)
    inner = jnp.tanh(GELU_C * (pre + GELU_A * pre * pre * pre))
    act_ref[:, HD:] = (0.5 * pre * (1.0 + inner)).astype(BF)


def part_of(offset, all_ref, w_attn_ref, w_mlp_ref, part):
    start = pl.multiple_of(image_of(offset) * PATCH, PATCH)
    rows = all_ref[pl.ds(start, PATCH), :]
    part[:, 0:HD] = dot(rows, w_attn_ref[...], 1, 1).astype(BF)
    part[:, HD:] = dot(rows, w_mlp_ref[...], 1, 1).astype(BF)


FIRST = [4, 7, 6, 1]
SECOND = [5, 2, 3, 0]


def spread_kernel(*refs):
    pieces, (w_attn_ref, w_mlp_ref, all_ref), parts = refs[:6], refs[6:9], refs[9:]
    own_pair, other_pair, mine_a, mine_b, theirs_a, theirs_b = pieces
    h, z, c = mp_place()
    step = 1 - 2 * c

    def put(piece, place_z, core):
        for dh in range(NH):
            spot = ((h + dh) % NH * NZ + (place_z + 2 * NZ) % NZ) * NC + core
            all_ref[pl.ds(pl.multiple_of(spot * ROWS, ROWS), ROWS), :] = piece[dh]

    put(own_pair, z, c)
    put(other_pair, z, 1 - c)
    for r in range(1, 5):
        put(mine_a.at[r - 1], z - step * r, c)
        put(theirs_a.at[r - 1], z + step * r, 1 - c)
        if r < 4:
            put(mine_b.at[r - 1], z - step * r, 1 - c)
            put(theirs_b.at[r - 1], z + step * r, c)
    for index, part in zip(FIRST, parts):
        part_of(OFFSETS[index], all_ref, w_attn_ref, w_mlp_ref, part)


def parts_kernel(all_ref, w_attn_ref, w_mlp_ref, *parts):
    for index, part in zip(SECOND, parts):
        part_of(OFFSETS[index], all_ref, w_attn_ref, w_mlp_ref, part)


def middle_kernel(qkv_ref, pre_ref, a_ref, b_ref, c_ref, d_ref, grad_ref):
    total = (
        a_ref[...].astype(F32)
        + b_ref[...].astype(F32)
        + c_ref[...].astype(F32)
        + d_ref[...].astype(F32)
    )
    upward = total[:, 0:HD].astype(BF)
    query, key, value = (qkv_ref[:, i * HD : (i + 1) * HD] for i in range(3))
    probs = attn_probs_of(query, key)
    rounded = probs.astype(BF)
    grad_value = dot(rounded, upward, 0, 0)
    grad_probs = dot(upward, value, 1, 1)
    centred = grad_probs - jnp.sum(grad_probs * probs, axis=-1, keepdims=True)
    grad_scores = (probs * centred * (HD**-0.5)).astype(BF)
    grad_ref[:, 0:HD] = dot(grad_scores, key, 1, 0).astype(BF)
    grad_ref[:, HD : 2 * HD] = dot(grad_scores, query, 0, 0).astype(BF)
    grad_ref[:, 2 * HD : 3 * HD] = grad_value.astype(BF)
    pre = pre_ref[...].astype(F32)
    inner = jnp.tanh(GELU_C * (pre + GELU_A * pre * pre * pre))
    slope = 0.5 * (1.0 + inner) + 0.5 * pre * (1.0 - inner * inner) * (
        GELU_C * (1.0 + 3.0 * GELU_A * pre * pre)
    )
    grad_ref[:, 3 * HD :] = (total[:, HD:] * slope).astype(BF)


def normed_rows(grad, w_qkv_ref, w_mlp_ref):
    rows = dot(grad[:, 0 : 3 * HD], w_qkv_ref[...], 1, 1) + dot(
        grad[:, 3 * HD :], w_mlp_ref[...], 1, 1
    )
    return rows.astype(BF)


def normed_kernel(*refs):
    grads, (w_qkv_ref, w_mlp_ref), outs = refs[:4], refs[4:6], refs[6:]
    for grad, out in zip(grads, outs):
        out[...] = normed_rows(grad, w_qkv_ref, w_mlp_ref)


def sort_kernel(*refs):
    ready, grads, (w_qkv_ref, w_mlp_ref, mine_ref, other_ref) = refs[:4], refs[4:8], refs[8:]
    h, z, c = mp_place()
    step = 1 - 2 * c

    def put(spot, dh, block):
        @pl.when(spot < 8)
        def _():
            mine_ref[spot, dh] = block

        @pl.when(spot >= 8)
        def _():
            other_ref[spot - 8, dh] = block

    for k, offset in enumerate(OFFSETS):
        image = image_of(offset)
        rows = ready[k] if k < 4 else normed_rows(grads[k - 4], w_qkv_ref, w_mlp_ref)
        dh = (image // 4 + h) % NH
        for half in range(2):
            ahead = ((image % 4 * 2 + half - z) * step + NZ) % NZ
            same = jnp.where(ahead <= 4, ahead, 20 - ahead)
            cross = jnp.where(ahead == 0, 8, jnp.where(ahead <= 3, 4 + ahead, 16 - ahead))
            for core in range(2):
                at = (half * 2 + core) * ROWS
                put(jnp.where(c == core, same, cross), dh, rows[at : at + ROWS])


def out_weights_kernel(*refs):
    acts, (all_ref, attn_ref, mlp_ref, acc_ref) = refs[:8], refs[8:]
    for k, (offset, act) in enumerate(zip(OFFSETS, acts)):
        start = pl.multiple_of(image_of(offset) * PATCH, PATCH)
        term = dot(act[...], all_ref[pl.ds(start, PATCH), :], 0, 0)
        if k == 0:
            acc_ref[...] = term
        else:
            acc_ref[...] += term
    attn_ref[...] = acc_ref[0:HD].astype(BF)
    mlp_ref[...] = acc_ref[HD:].astype(BF)


def in_weights_kernel(*refs):
    grads, (all_ref, w_qkv_ref, w_mlp_ref, qkv_ref, mlp_ref, gain_ref, acc_ref) = (
        refs[:8],
        refs[8:],
    )
    for k, (offset, grad) in enumerate(zip(OFFSETS, grads)):
        start = pl.multiple_of(image_of(offset) * PATCH, PATCH)
        term = dot(all_ref[pl.ds(start, PATCH), :], grad[...], 0, 0)
        if k == 0:
            acc_ref[...] = term
        else:
            acc_ref[...] += term
    qkv = acc_ref[:, 0 : 3 * HD]
    mlp = acc_ref[:, 3 * HD :]
    qkv_ref[...] = qkv.astype(BF)
    mlp_ref[...] = mlp.astype(BF)
    gain_ref[...] = jnp.sum(qkv * w_qkv_ref[...].astype(F32), axis=1, keepdims=True) + jnp.sum(
        mlp * w_mlp_ref[...].astype(F32), axis=1, keepdims=True
    )


def add(*terms):
    total = terms[0].astype(F32)
    for term in terms[1:]:
        total = total + term.astype(F32)
    return total.astype(BF)


def gather_dp(own):
    below, above, beside = lax.optimization_barrier(
        (dp_send(own, Y_UP), dp_send(own, Y_DOWN), dp_send(own, X_SWAP))
    )
    beside_above = dp_send(beside, Y_DOWN)
    beside_below = dp_send(beside, Y_UP)
    far = dp_send(below, Y_UP)
    beside_far = dp_send(beside_above, Y_DOWN)
    return [own, above, below, beside, far, beside_above, beside_below, beside_far]


def scatter_dp(parts):
    own, above, below, beside, far, beside_above, beside_below, beside_far = parts
    down = dp_send(far, Y_DOWN)
    up = dp_send(beside_far, Y_UP)
    down_beside = dp_send(beside_below, Y_DOWN)
    up_beside = dp_send(add(beside_above, up), Y_UP)
    down_last = dp_send(add(below, down), Y_DOWN)
    up_last = dp_send(above, Y_UP)
    across = dp_send(add(beside, down_beside, up_beside), X_SWAP)
    return own, down_last, up_last, across


def gather_mp(own, act):
    own_pair = jnp.stack([own, mp_send(own, H_SWAP)])
    own_pair, act = lax.optimization_barrier((own_pair, act))
    all_acts = gather_dp(act)
    other_pair = mp_send(own_pair, C_SWAP)
    mine_a, mine_b = [own_pair], [other_pair]
    for step in range(4):
        mine_a.append(mp_send(mine_a[-1], Z_RING))
        if step < 3:
            mine_b.append(mp_send(mine_b[-1], Z_RING))
    mine_a, mine_b = jnp.stack(mine_a[1:]), jnp.stack(mine_b[1:])
    theirs_b = mp_send(mine_b, C_SWAP)
    theirs_a = mp_send(mine_a, C_SWAP)
    return [own_pair, other_pair, mine_a, mine_b, theirs_a, theirs_b], all_acts


def scatter_mp(mine, other, tied):
    received = mp_send(other, C_SWAP)
    ring_a = mp_send(add(mine[4], received[4]), Z_RING)
    ring_b = mp_send(add(mine[7], received[7]), Z_RING)
    ring_a = mp_send(add(mine[3], received[3], ring_a), Z_RING)
    ring_b = mp_send(add(mine[6], received[6], ring_b), Z_RING)
    ring_a, tied = lax.optimization_barrier((ring_a, tied))
    ring_a = mp_send(add(mine[2], received[2], ring_a), Z_RING)
    ring_b = mp_send(add(mine[5], received[5], ring_b), Z_RING)
    ring_a = mp_send(add(mine[1], received[1], ring_a), Z_RING)
    ring_b = mp_send(ring_b, C_SWAP)
    gain = tied[2]
    for perm in (C_SWAP, H_SWAP):
        gain = gain + mp_send(gain, perm)
    ring_a, gain = lax.optimization_barrier((ring_a, gain))
    across = mp_send(add(mine[0, 1], received[0, 1], ring_a[1], ring_b[1]), H_SWAP)
    total = across.astype(F32)
    for term in (mine, received):
        total = total + term[0, 0].astype(F32)
    return total + ring_a[0].astype(F32) + ring_b[0].astype(F32), tied[:2], gain


def sum_dp(values):
    for perm in (X_SWAP, Y_ONE, Y_TWO):
        values = values + dp_send(values, perm)
    return values


def per_device(
    block_input, ln_gain, qkv_act, mlp_pre, out_grad, w_qkv, w_mlp, w_out_attn, w_out_mlp
):
    width = block_input.shape[1]
    shape = jax.ShapeDtypeStruct
    widened = block_input.astype(F32)
    mean = jnp.mean(widened, axis=1)
    square = jnp.sum(jnp.square(widened - mean[:, None]), axis=1)
    count = width
    for perm in (X_SWAP, Y_ONE, Y_TWO):
        theirs = dp_send(jnp.stack([mean, square]), perm)
        gap = mean - theirs[0]
        square = square + theirs[1] + gap * gap * (count / 2)
        mean = (mean + theirs[0]) * 0.5
        count = count * 2
    inverse = lax.rsqrt(square / D + eps)
    normed = (widened - mean[:, None]) * inverse[:, None]
    scaled = (normed * ln_gain[None, :]).astype(BF)
    act = call(
        forward_kernel, shape((PATCH, 896), BF), 2, flops=10**8, nbytes=2 * 10**6
    )(qkv_act, mlp_pre)
    pieces, all_acts = gather_mp(out_grad, act)
    pieces, scaled, all_acts = lax.optimization_barrier((pieces, scaled, all_acts))
    all_scaled = lax.all_gather(scaled, "mp", axis=0, tiled=True)
    part_shape = [shape((PATCH, 896), BF)] * 4
    all_grad, *first = call(
        spread_kernel,
        [shape((2048, 768), BF)] + part_shape,
        8,
        flops=2048 * 768 * 896,
        nbytes=10 * 10**6,
    )(*pieces, w_out_attn, w_out_mlp)
    second = call(parts_kernel, part_shape, 3, flops=2048 * 768 * 896, nbytes=6 * 10**6)(
        all_grad, w_out_attn, w_out_mlp
    )
    parts = [None] * 8
    for index, part in zip(FIRST + SECOND, first + list(second)):
        parts[index] = part
    sums = scatter_dp(parts)
    grad = call(
        middle_kernel, shape((PATCH, 1152), BF), 6, flops=2 * 10**8, nbytes=3 * 10**6
    )(qkv_act, mlp_pre, *sums)
    grads = gather_dp(grad)
    acc_attn, acc_mlp = call(
        out_weights_kernel,
        [shape((HD, 768), BF), shape((768, 768), BF)],
        9,
        scratch=[pltpu.VMEM((896, 768), F32)],
        flops=2 * 2048 * 768 * 896,
        nbytes=8 * 10**6,
    )(*all_acts, all_grad)
    early, late = grads[:4], grads[4:]
    ready = call(
        normed_kernel,
        [shape((PATCH, 768), BF)] * 4,
        6,
        flops=2048 * 768 * 1152,
        nbytes=6 * 10**6,
    )(*early, w_qkv, w_mlp)
    late, all_scaled, acc_attn, acc_mlp = lax.optimization_barrier(
        (late, all_scaled, acc_attn, acc_mlp)
    )
    mine, other = call(
        sort_kernel,
        [shape((8, NH, ROWS, 768), BF)] * 2,
        10,
        flops=2048 * 768 * 1152,
        nbytes=8 * 10**6,
    )(*ready, *late, w_qkv, w_mlp)
    acc_qkv, acc_pre, gain_part = call(
        in_weights_kernel,
        [shape((768, 384), BF), shape((768, 768), BF), shape((768, 1), F32)],
        11,
        scratch=[pltpu.VMEM((768, 1152), F32)],
        flops=2 * 2048 * 768 * 1152,
        nbytes=11 * 10**6,
    )(*grads, all_scaled, w_qkv, w_mlp)
    grad_normed, (acc_qkv, acc_pre), gain_grad = scatter_mp(
        mine, other, (acc_qkv, acc_pre, gain_part[:, 0] / ln_gain)
    )
    for perm in Z_XOR:
        gain_grad = gain_grad + mp_send(gain_grad, perm)
    weighted = grad_normed * ln_gain[None, :]
    sums = sum_dp(jnp.stack([jnp.sum(weighted, axis=1), jnp.sum(weighted * normed, axis=1)])) / D
    input_grad = out_grad.astype(F32) + inverse[:, None] * (
        weighted - sums[0][:, None] - normed * sums[1][:, None]
    )
    return (input_grad.astype(BF), acc_qkv, acc_pre, acc_attn, acc_mlp, gain_grad)


def solution(mesh):
    return jax.shard_map(
        per_device,
        mesh=mesh,
        in_specs=(
            P("mp", "dp"),
            P("dp"),
            P("dp", "mp"),
            P("dp", "mp"),
            P("mp", "dp"),
            P("dp", "mp"),
            P("dp", "mp"),
            P("mp", "dp"),
            P("mp", "dp"),
        ),
        out_specs=(
            P("mp", "dp"),
            P("dp", "mp"),
            P("dp", "mp"),
            P("mp", "dp"),
            P("mp", "dp"),
            P("dp"),
        ),
        check_vma=False,
    )
```

```python
import functools
import jax
import jax.numpy as jnp
from jax import lax
from jax.experimental import pallas as pl
from jax.experimental.pallas import tpu as pltpu
from jax.sharding import PartitionSpec as P

D = 6144
HD = 128
PATCH = 256
eps = 1e-06
BF = jnp.bfloat16
F32 = jnp.float32

NY, NX, NH, NZ, NC = 4, 2, 2, 8, 2
ROWS = 64


def dp_perm(move):
    pairs = []
    for y in range(NY):
        for x in range(NX):
            to_y, to_x = move(y, x)
            pairs.append((y * NX + x, (to_y % NY) * NX + to_x))
    return pairs


def mp_perm(move):
    pairs = []
    for h in range(NH):
        for z in range(NZ):
            for c in range(NC):
                to_h, to_z, to_c = move(h, z, c)
                pairs.append(((h * NZ + z) * NC + c, (to_h * NZ + to_z % NZ) * NC + to_c))
    return pairs


X_SWAP = dp_perm(lambda y, x: (y, 1 - x))
Y_UP = dp_perm(lambda y, x: (y + 1, x))
Y_DOWN = dp_perm(lambda y, x: (y - 1, x))
Y_ONE = dp_perm(lambda y, x: (y ^ 1, x))
Y_TWO = dp_perm(lambda y, x: (y ^ 2, x))
H_SWAP = mp_perm(lambda h, z, c: (1 - h, z, c))
C_SWAP = mp_perm(lambda h, z, c: (h, z, 1 - c))
Z_RING = mp_perm(lambda h, z, c: (h, z + 1 - 2 * c, c))
Z_XOR = [mp_perm(functools.partial(lambda bit, h, z, c: (h, z ^ bit, c), bit)) for bit in (1, 2, 4)]

OFFSETS = [(0, 0), (1, 0), (3, 0), (0, 1), (2, 0), (1, 1), (3, 1), (2, 1)]


def dp_send(array, perm):
    return lax.ppermute(array, "dp", perm)


def mp_send(array, perm):
    return lax.ppermute(array, "mp", perm)


def dp_place():
    index = lax.axis_index("dp")
    return index // NX, index % NX


def mp_place():
    index = lax.axis_index("mp")
    return index // (NZ * NC), (index // NC) % NZ, index % NC


def image_of(offset):
    y, x = dp_place()
    dy, dx = offset
    return ((y + dy) % NY) * NX + (x + dx) % NX


def dot(a, b, ca, cb):
    return lax.dot_general(a, b, (((ca,), (cb,)), ((), ())), preferred_element_type=F32)


def call(kernel, out_shape, n_in, limit, flops=0, nbytes=0, scratch=(), any_in=(), any_out=False, aliases={}):
    specs = [
        pl.BlockSpec(memory_space=pl.ANY if i in any_in else pltpu.VMEM) for i in range(n_in)
    ]
    out_space = pl.ANY if any_out else pltpu.VMEM
    outs = jax.tree.map(lambda _: pl.BlockSpec(memory_space=out_space), out_shape)
    return pl.pallas_call(
        kernel,
        out_shape=out_shape,
        in_specs=specs,
        out_specs=outs,
        scratch_shapes=list(scratch),
        input_output_aliases=aliases,
        compiler_params=pltpu.CompilerParams(vmem_limit_bytes=limit * 1024 * 1024),
        cost_estimate=pl.CostEstimate(flops=flops, bytes_accessed=nbytes, transcendentals=0),
    )


GELU_C = 0.7978845608028654
GELU_A = 0.044715


def attn_probs_of(query, key):
    scores = dot(query, key, 1, 1) * (HD**-0.5)
    scores = scores - jnp.max(scores, axis=-1, keepdims=True)
    powers = jnp.exp(scores)
    return powers / jnp.sum(powers, axis=-1, keepdims=True)


def forward_kernel(qkv_ref, pre_ref, act_ref):
    probs = attn_probs_of(qkv_ref[:, 0:HD], qkv_ref[:, HD : 2 * HD])
    attended = dot(probs.astype(BF), qkv_ref[:, 2 * HD : 3 * HD], 1, 0)
    act_ref[:, 0:HD] = attended.astype(BF)
    pre = pre_ref[...].astype(F32)
    inner = jnp.tanh(GELU_C * (pre + GELU_A * pre * pre * pre))
    act_ref[:, HD:] = (0.5 * pre * (1.0 + inner)).astype(BF)


def part_of(offset, all_ref, w_attn_ref, w_mlp_ref, part):
    start = pl.multiple_of(image_of(offset) * PATCH, PATCH)
    rows = all_ref[pl.ds(start, PATCH), :]
    part[:, 0:HD] = dot(rows, w_attn_ref[...], 1, 1).astype(BF)
    part[:, HD:] = dot(rows, w_mlp_ref[...], 1, 1).astype(BF)


FIRST = [4, 7, 6, 1]
SECOND = [5, 2, 3, 0]


def spread_kernel(*refs):
    pieces, (w_attn_ref, w_mlp_ref, all_ref), parts = refs[:6], refs[6:9], refs[9:]
    own_pair, other_pair, mine, last, theirs, theirs_last = pieces
    h, z, c = mp_place()
    step = 1 - 2 * c

    def put(piece, place_z, core):
        for dh in range(NH):
            spot = ((h + dh) % NH * NZ + (place_z + 2 * NZ) % NZ) * NC + core
            all_ref[pl.ds(pl.multiple_of(spot * ROWS, ROWS), ROWS), :] = piece[dh]

    put(own_pair, z, c)
    put(other_pair, z, 1 - c)
    put(last, z - step * 4, c)
    put(theirs_last, z + step * 4, 1 - c)
    for r in range(1, 4):
        put(mine.at[r - 1], z - step * r, c)
        put(theirs.at[r - 1], z + step * r, 1 - c)
        put(mine.at[r + 2], z - step * r, 1 - c)
        put(theirs.at[r + 2], z + step * r, c)
    for index, part in zip(FIRST, parts):
        part_of(OFFSETS[index], all_ref, w_attn_ref, w_mlp_ref, part)


def parts_kernel(all_ref, w_attn_ref, w_mlp_ref, *parts):
    for index, part in zip(SECOND, parts):
        part_of(OFFSETS[index], all_ref, w_attn_ref, w_mlp_ref, part)


def middle_kernel(qkv_ref, pre_ref, a_ref, b_ref, c_ref, d_ref, grad_ref):
    total = (
        a_ref[...].astype(F32)
        + b_ref[...].astype(F32)
        + c_ref[...].astype(F32)
        + d_ref[...].astype(F32)
    )
    upward = total[:, 0:HD].astype(BF)
    query, key, value = (qkv_ref[:, i * HD : (i + 1) * HD] for i in range(3))
    probs = attn_probs_of(query, key)
    rounded = probs.astype(BF)
    grad_value = dot(rounded, upward, 0, 0)
    grad_probs = dot(upward, value, 1, 1)
    centred = grad_probs - jnp.sum(grad_probs * probs, axis=-1, keepdims=True)
    grad_scores = (probs * centred * (HD**-0.5)).astype(BF)
    grad_ref[:, 0:HD] = dot(grad_scores, key, 1, 0).astype(BF)
    grad_ref[:, HD : 2 * HD] = dot(grad_scores, query, 0, 0).astype(BF)
    grad_ref[:, 2 * HD : 3 * HD] = grad_value.astype(BF)
    pre = pre_ref[...].astype(F32)
    inner = jnp.tanh(GELU_C * (pre + GELU_A * pre * pre * pre))
    slope = 0.5 * (1.0 + inner) + 0.5 * pre * (1.0 - inner * inner) * (
        GELU_C * (1.0 + 3.0 * GELU_A * pre * pre)
    )
    grad_ref[:, 3 * HD :] = (total[:, HD:] * slope).astype(BF)


def sort_rows(grads, offsets, w_qkv_ref, w_mlp_ref, mine_ref, other_ref, rows_ref, sem):
    h, z, c = mp_place()
    step = 1 - 2 * c
    moves = []
    for k, (grad, offset) in enumerate(zip(grads, offsets)):
        image = image_of(offset)
        rows = dot(grad[:, 0 : 3 * HD], w_qkv_ref[...], 1, 1) + dot(
            grad[:, 3 * HD :], w_mlp_ref[...], 1, 1
        )
        rows_ref[k] = rows.astype(BF)
        dh = (image // 4 + h) % NH
        for half in range(2):
            ahead = ((image % 4 * 2 + half - z) * step + NZ) % NZ
            same = jnp.where(ahead <= 4, ahead, 20 - ahead)
            cross = jnp.where(ahead == 0, 8, jnp.where(ahead <= 3, 4 + ahead, 16 - ahead))
            for core in range(2):
                spot = jnp.where(c == core, same, cross)
                index = half * 2 + core
                source = rows_ref.at[k, pl.ds(index * ROWS, ROWS)]
                moves.append((spot, dh, source, sem.at[k, index]))
                move(moves[-1], mine_ref, other_ref, True)
    for one in moves:
        move(one, mine_ref, other_ref, False)


def move(one, mine_ref, other_ref, start):
    spot, dh, source, sem = one

    @pl.when(spot < 8)
    def _():
        copy = pltpu.make_async_copy(source, mine_ref.at[spot, dh], sem)
        copy.start() if start else copy.wait()

    @pl.when(spot >= 8)
    def _():
        copy = pltpu.make_async_copy(source, other_ref.at[spot - 8, dh], sem)
        copy.start() if start else copy.wait()


def early_kernel(*refs):
    sort_rows(refs[:4], OFFSETS[:4], *refs[4:])


def late_kernel(*refs):
    sort_rows(refs[2:6], OFFSETS[4:], *refs[6:])


def out_weights_kernel(*refs):
    acts, (all_ref, attn_ref, mlp_ref, acc_ref) = refs[:8], refs[8:]
    for k, (offset, act) in enumerate(zip(OFFSETS, acts)):
        start = pl.multiple_of(image_of(offset) * PATCH, PATCH)
        term = dot(act[...], all_ref[pl.ds(start, PATCH), :], 0, 0)
        if k == 0:
            acc_ref[...] = term
        else:
            acc_ref[...] += term
    attn_ref[...] = acc_ref[0:HD].astype(BF)
    mlp_ref[...] = acc_ref[HD:].astype(BF)


def in_early_kernel(*refs):
    grads, (all_ref, acc_ref) = refs[:4], refs[4:]
    for k, (offset, grad) in enumerate(zip(OFFSETS[:4], grads)):
        start = pl.multiple_of(image_of(offset) * PATCH, PATCH)
        term = dot(all_ref[pl.ds(start, PATCH), :], grad[...], 0, 0)
        if k == 0:
            acc_ref[...] = term
        else:
            acc_ref[...] += term


def in_late_kernel(*refs):
    grads, (all_ref, half_ref, w_qkv_ref, w_mlp_ref, qkv_ref, mlp_ref, gain_ref, acc_ref) = (
        refs[:4],
        refs[4:],
    )
    for k, (offset, grad) in enumerate(zip(OFFSETS[4:], grads)):
        start = pl.multiple_of(image_of(offset) * PATCH, PATCH)
        term = dot(all_ref[pl.ds(start, PATCH), :], grad[...], 0, 0)
        if k == 0:
            acc_ref[...] = half_ref[...] + term
        else:
            acc_ref[...] += term
    qkv = acc_ref[:, 0 : 3 * HD]
    mlp = acc_ref[:, 3 * HD :]
    qkv_ref[...] = qkv.astype(BF)
    mlp_ref[...] = mlp.astype(BF)
    gain_ref[...] = jnp.sum(qkv * w_qkv_ref[...].astype(F32), axis=1, keepdims=True) + jnp.sum(
        mlp * w_mlp_ref[...].astype(F32), axis=1, keepdims=True
    )


def add(*terms):
    total = terms[0].astype(F32)
    for term in terms[1:]:
        total = total + term.astype(F32)
    return total.astype(BF)


def gather_dp_first(own):
    return dp_send(own, Y_UP), dp_send(own, Y_DOWN), dp_send(own, X_SWAP)


def gather_dp_rest(own, below, above, beside):
    beside_above = dp_send(beside, Y_DOWN)
    beside_below = dp_send(beside, Y_UP)
    far = dp_send(below, Y_UP)
    beside_far = dp_send(beside_above, Y_DOWN)
    return [own, above, below, beside, far, beside_above, beside_below, beside_far]


def scatter_dp(parts):
    own, above, below, beside, far, beside_above, beside_below, beside_far = parts
    down = dp_send(far, Y_DOWN)
    up = dp_send(beside_far, Y_UP)
    down_beside = dp_send(beside_below, Y_DOWN)
    up_beside = dp_send(add(beside_above, up), Y_UP)
    down_last = dp_send(add(below, down), Y_DOWN)
    up_last = dp_send(above, Y_UP)
    across = dp_send(add(beside, down_beside, up_beside), X_SWAP)
    return own, down_last, up_last, across


def gather_mp(own, act, scaled):
    own_pair = jnp.stack([own, mp_send(own, H_SWAP)])
    own_pair, act = lax.optimization_barrier((own_pair, act))
    first = gather_dp_first(act)
    other_pair = mp_send(own_pair, C_SWAP)
    mine_a, mine_b = [mp_send(own_pair, Z_RING)], [mp_send(other_pair, Z_RING)]
    mine_a.append(mp_send(mine_a[-1], Z_RING))
    mine_a, mine_b, first, scaled = lax.optimization_barrier((mine_a, mine_b, first, scaled))
    for _ in range(2):
        mine_a.append(mp_send(mine_a[-1], Z_RING))
        mine_b.append(mp_send(mine_b[-1], Z_RING))
    mine = jnp.stack(mine_a[:3] + mine_b)
    last = mine_a[3]
    theirs, theirs_last = mp_send(mine, C_SWAP), mp_send(last, C_SWAP)
    all_acts = gather_dp_rest(act, *first)
    return [own_pair, other_pair, mine, last, theirs, theirs_last], all_acts, scaled


def scatter_mp(mine, other, tied):
    held = add(mine, mp_send(other, C_SWAP))
    ring_a = mp_send(held[4], Z_RING)
    ring_b = mp_send(held[7], Z_RING)
    ring_a = mp_send(add(held[3], ring_a), Z_RING)
    ring_b = mp_send(add(held[6], ring_b), Z_RING)
    ring_a, tied = lax.optimization_barrier((ring_a, tied))
    gain = tied[2]
    ring_a = mp_send(add(held[2], ring_a), Z_RING)
    ring_b = mp_send(add(held[5], ring_b), Z_RING)
    for perm in (C_SWAP, H_SWAP, Z_XOR[0]):
        gain = gain + mp_send(gain, perm)
    ring_a = mp_send(add(held[1], ring_a), Z_RING)
    ring_b = mp_send(ring_b, C_SWAP)
    ring_a, gain = lax.optimization_barrier((ring_a, gain))
    across = mp_send(add(held[0, 1], ring_a[1], ring_b[1]), H_SWAP)
    total = across.astype(F32)
    for term in (held[0, 0], ring_a[0], ring_b[0]):
        total = total + term.astype(F32)
    for perm in Z_XOR[1:]:
        gain = gain + mp_send(gain, perm)
    return total, tied[:2], gain


def sum_dp(values):
    for perm in (X_SWAP, Y_ONE, Y_TWO):
        values = values + dp_send(values, perm)
    return values


def per_device(
    block_input, ln_gain, qkv_act, mlp_pre, out_grad, w_qkv, w_mlp, w_out_attn, w_out_mlp
):
    width = block_input.shape[1]
    shape = jax.ShapeDtypeStruct
    widened = block_input.astype(F32)
    mean = jnp.mean(widened, axis=1)
    square = jnp.sum(jnp.square(widened - mean[:, None]), axis=1)
    count = width
    for perm in (X_SWAP, Y_ONE, Y_TWO):
        theirs = dp_send(jnp.stack([mean, square]), perm)
        gap = mean - theirs[0]
        square = square + theirs[1] + gap * gap * (count / 2)
        mean = (mean + theirs[0]) * 0.5
        count = count * 2
    inverse = lax.rsqrt(square / D + eps)
    normed = (widened - mean[:, None]) * inverse[:, None]
    scaled = (normed * ln_gain[None, :]).astype(BF)
    act = call(
        forward_kernel, shape((PATCH, 896), BF), 2, 10, flops=10**8, nbytes=2 * 10**6
    )(qkv_act, mlp_pre)
    pieces, all_acts, scaled = gather_mp(out_grad, act, scaled)
    all_scaled = lax.all_gather(scaled, "mp", axis=0, tiled=True)
    pieces, all_acts = lax.optimization_barrier((pieces, all_acts))
    part_shape = [shape((PATCH, 896), BF)] * 4
    all_grad, *first = call(
        spread_kernel,
        [shape((2048, 768), BF)] + part_shape,
        8,
        16,
        flops=2048 * 768 * 896,
        nbytes=10 * 10**6,
    )(*pieces, w_out_attn, w_out_mlp)
    second = call(parts_kernel, part_shape, 3, 14, flops=2048 * 768 * 896, nbytes=6 * 10**6)(
        all_grad, w_out_attn, w_out_mlp
    )
    parts = [None] * 8
    for index, part in zip(FIRST + SECOND, first + list(second)):
        parts[index] = part
    sums = scatter_dp(parts)
    grad = call(
        middle_kernel, shape((PATCH, 1152), BF), 6, 14, flops=2 * 10**8, nbytes=3 * 10**6
    )(qkv_act, mlp_pre, *sums)
    near = gather_dp_first(grad)
    acc_attn, acc_mlp = call(
        out_weights_kernel,
        [shape((HD, 768), BF), shape((768, 768), BF)],
        9,
        22,
        scratch=[pltpu.VMEM((896, 768), F32)],
        flops=2 * 2048 * 768 * 896,
        nbytes=8 * 10**6,
    )(*all_acts, all_grad)
    near, all_scaled, acc_attn, acc_mlp = lax.optimization_barrier(
        (near, all_scaled, acc_attn, acc_mlp)
    )
    grads = gather_dp_rest(grad, *near)
    early, late = grads[:4], grads[4:]
    slots = [shape((8, NH, ROWS, 768), BF)] * 2
    sort_scratch = [pltpu.VMEM((4, PATCH, 768), BF), pltpu.SemaphoreType.DMA((4, 4))]
    mine, other = call(
        early_kernel,
        slots,
        6,
        16,
        flops=2048 * 768 * 1152,
        nbytes=6 * 10**6,
        scratch=sort_scratch,
        any_out=True,
    )(*early, w_qkv, w_mlp)
    acc_half = call(
        in_early_kernel,
        shape((768, 1152), F32),
        5,
        18,
        flops=2048 * 768 * 1152,
        nbytes=9 * 10**6,
    )(*early, all_scaled)
    late, acc_half = lax.optimization_barrier((late, acc_half))
    mine, other = call(
        late_kernel,
        slots,
        8,
        16,
        flops=2048 * 768 * 1152,
        nbytes=6 * 10**6,
        scratch=sort_scratch,
        any_in=(0, 1),
        any_out=True,
        aliases={0: 0, 1: 1},
    )(mine, other, *late, w_qkv, w_mlp)
    acc_qkv, acc_pre, gain_part = call(
        in_late_kernel,
        [shape((768, 384), BF), shape((768, 768), BF), shape((768, 1), F32)],
        8,
        24,
        scratch=[pltpu.VMEM((768, 1152), F32)],
        flops=2048 * 768 * 1152,
        nbytes=12 * 10**6,
    )(*late, all_scaled, acc_half, w_qkv, w_mlp)
    grad_normed, (acc_qkv, acc_pre), gain_grad = scatter_mp(
        mine, other, (acc_qkv, acc_pre, gain_part[:, 0] / ln_gain)
    )
    weighted = grad_normed * ln_gain[None, :]
    sums = sum_dp(jnp.stack([jnp.sum(weighted, axis=1), jnp.sum(weighted * normed, axis=1)])) / D
    input_grad = out_grad.astype(F32) + inverse[:, None] * (
        weighted - sums[0][:, None] - normed * sums[1][:, None]
    )
    return (input_grad.astype(BF), acc_qkv, acc_pre, acc_attn, acc_mlp, gain_grad)


def solution(mesh):
    return jax.shard_map(
        per_device,
        mesh=mesh,
        in_specs=(
            P("mp", "dp"),
            P("dp"),
            P("dp", "mp"),
            P("dp", "mp"),
            P("mp", "dp"),
            P("dp", "mp"),
            P("dp", "mp"),
            P("mp", "dp"),
            P("mp", "dp"),
        ),
        out_specs=(
            P("mp", "dp"),
            P("dp", "mp"),
            P("dp", "mp"),
            P("mp", "dp"),
            P("mp", "dp"),
            P("dp"),
        ),
        check_vma=False,
    )
```

```python
import functools
import jax
import jax.numpy as jnp
from jax import lax
from jax.experimental import pallas as pl
from jax.experimental.pallas import tpu as pltpu
from jax.sharding import PartitionSpec as P

D = 6144
HD = 128
PATCH = 256
eps = 1e-06
BF = jnp.bfloat16
F32 = jnp.float32

NY, NX, NH, NZ, NC = 4, 2, 2, 8, 2
ROWS = 64


def dp_perm(move):
    pairs = []
    for y in range(NY):
        for x in range(NX):
            to_y, to_x = move(y, x)
            pairs.append((y * NX + x, (to_y % NY) * NX + to_x))
    return pairs


def mp_perm(move):
    pairs = []
    for h in range(NH):
        for z in range(NZ):
            for c in range(NC):
                to_h, to_z, to_c = move(h, z, c)
                pairs.append(((h * NZ + z) * NC + c, (to_h * NZ + to_z % NZ) * NC + to_c))
    return pairs


X_SWAP = dp_perm(lambda y, x: (y, 1 - x))
Y_UP = dp_perm(lambda y, x: (y + 1, x))
Y_DOWN = dp_perm(lambda y, x: (y - 1, x))
Y_ONE = dp_perm(lambda y, x: (y ^ 1, x))
Y_TWO = dp_perm(lambda y, x: (y ^ 2, x))
H_SWAP = mp_perm(lambda h, z, c: (1 - h, z, c))
C_SWAP = mp_perm(lambda h, z, c: (h, z, 1 - c))
Z_RING = mp_perm(lambda h, z, c: (h, z + 1 - 2 * c, c))
Z_XOR = [mp_perm(functools.partial(lambda bit, h, z, c: (h, z ^ bit, c), bit)) for bit in (1, 2, 4)]

OFFSETS = [(0, 0), (1, 0), (3, 0), (0, 1), (2, 0), (1, 1), (3, 1), (2, 1)]


def dp_send(array, perm):
    return lax.ppermute(array, "dp", perm)


def mp_send(array, perm):
    return lax.ppermute(array, "mp", perm)


def dp_place():
    index = lax.axis_index("dp")
    return index // NX, index % NX


def mp_place():
    index = lax.axis_index("mp")
    return index // (NZ * NC), (index // NC) % NZ, index % NC


def image_of(offset):
    y, x = dp_place()
    dy, dx = offset
    return ((y + dy) % NY) * NX + (x + dx) % NX


def dot(a, b, ca, cb):
    return lax.dot_general(a, b, (((ca,), (cb,)), ((), ())), preferred_element_type=F32)


def call(kernel, out_shape, n_in, limit, flops=0, nbytes=0, scratch=(), any_in=(), any_out=False, aliases={}):
    specs = [
        pl.BlockSpec(memory_space=pl.ANY if i in any_in else pltpu.VMEM) for i in range(n_in)
    ]
    out_space = pl.ANY if any_out else pltpu.VMEM
    outs = jax.tree.map(lambda _: pl.BlockSpec(memory_space=out_space), out_shape)
    return pl.pallas_call(
        kernel,
        out_shape=out_shape,
        in_specs=specs,
        out_specs=outs,
        scratch_shapes=list(scratch),
        input_output_aliases=aliases,
        compiler_params=pltpu.CompilerParams(vmem_limit_bytes=limit * 1024 * 1024),
        cost_estimate=pl.CostEstimate(flops=flops, bytes_accessed=nbytes, transcendentals=0),
    )


GELU_C = 0.7978845608028654
GELU_A = 0.044715


def attn_probs_of(query, key):
    scores = dot(query, key, 1, 1) * (HD**-0.5)
    scores = scores - jnp.max(scores, axis=-1, keepdims=True)
    powers = jnp.exp(scores)
    return powers / jnp.sum(powers, axis=-1, keepdims=True)


def forward_kernel(qkv_ref, pre_ref, act_ref):
    probs = attn_probs_of(qkv_ref[:, 0:HD], qkv_ref[:, HD : 2 * HD])
    attended = dot(probs.astype(BF), qkv_ref[:, 2 * HD : 3 * HD], 1, 0)
    act_ref[:, 0:HD] = attended.astype(BF)
    pre = pre_ref[...].astype(F32)
    inner = jnp.tanh(GELU_C * (pre + GELU_A * pre * pre * pre))
    act_ref[:, HD:] = (0.5 * pre * (1.0 + inner)).astype(BF)


def part_of(offset, all_ref, w_attn_ref, w_mlp_ref, part):
    start = pl.multiple_of(image_of(offset) * PATCH, PATCH)
    rows = all_ref[pl.ds(start, PATCH), :]
    part[:, 0:HD] = dot(rows, w_attn_ref[...], 1, 1).astype(BF)
    part[:, HD:] = dot(rows, w_mlp_ref[...], 1, 1).astype(BF)


FIRST = [4, 7, 6, 1]
SECOND = [5, 2, 3, 0]


def spread_kernel(*refs):
    pieces, (w_attn_ref, w_mlp_ref, all_ref), parts = refs[:6], refs[6:9], refs[9:]
    own_pair, other_pair, mine, last, theirs, theirs_last = pieces
    h, z, c = mp_place()
    step = 1 - 2 * c

    def put(piece, place_z, core):
        for dh in range(NH):
            spot = ((h + dh) % NH * NZ + (place_z + 2 * NZ) % NZ) * NC + core
            all_ref[pl.ds(pl.multiple_of(spot * ROWS, ROWS), ROWS), :] = piece[dh]

    put(own_pair, z, c)
    put(other_pair, z, 1 - c)
    put(last, z - step * 4, c)
    put(theirs_last, z + step * 4, 1 - c)
    for r in range(1, 4):
        put(mine.at[r - 1], z - step * r, c)
        put(theirs.at[r - 1], z + step * r, 1 - c)
        put(mine.at[r + 2], z - step * r, 1 - c)
        put(theirs.at[r + 2], z + step * r, c)
    for index, part in zip(FIRST, parts):
        part_of(OFFSETS[index], all_ref, w_attn_ref, w_mlp_ref, part)


def parts_kernel(all_ref, w_attn_ref, w_mlp_ref, *parts):
    for index, part in zip(SECOND, parts):
        part_of(OFFSETS[index], all_ref, w_attn_ref, w_mlp_ref, part)


def middle_kernel(qkv_ref, pre_ref, a_ref, b_ref, c_ref, d_ref, grad_ref):
    total = (
        a_ref[...].astype(F32)
        + b_ref[...].astype(F32)
        + c_ref[...].astype(F32)
        + d_ref[...].astype(F32)
    )
    upward = total[:, 0:HD].astype(BF)
    query, key, value = (qkv_ref[:, i * HD : (i + 1) * HD] for i in range(3))
    probs = attn_probs_of(query, key)
    rounded = probs.astype(BF)
    grad_value = dot(rounded, upward, 0, 0)
    grad_probs = dot(upward, value, 1, 1)
    centred = grad_probs - jnp.sum(grad_probs * probs, axis=-1, keepdims=True)
    grad_scores = (probs * centred * (HD**-0.5)).astype(BF)
    grad_ref[:, 0:HD] = dot(grad_scores, key, 1, 0).astype(BF)
    grad_ref[:, HD : 2 * HD] = dot(grad_scores, query, 0, 0).astype(BF)
    grad_ref[:, 2 * HD : 3 * HD] = grad_value.astype(BF)
    pre = pre_ref[...].astype(F32)
    inner = jnp.tanh(GELU_C * (pre + GELU_A * pre * pre * pre))
    slope = 0.5 * (1.0 + inner) + 0.5 * pre * (1.0 - inner * inner) * (
        GELU_C * (1.0 + 3.0 * GELU_A * pre * pre)
    )
    grad_ref[:, 3 * HD :] = (total[:, HD:] * slope).astype(BF)


def sort_rows(grads, offsets, w_qkv_ref, w_mlp_ref, mine_ref, other_ref, rows_ref, sem):
    h, z, c = mp_place()
    step = 1 - 2 * c
    moves = []
    for k, (grad, offset) in enumerate(zip(grads, offsets)):
        image = image_of(offset)
        rows = dot(grad[:, 0 : 3 * HD], w_qkv_ref[...], 1, 1) + dot(
            grad[:, 3 * HD :], w_mlp_ref[...], 1, 1
        )
        rows_ref[k] = rows.astype(BF)
        dh = (image // 4 + h) % NH
        for half in range(2):
            ahead = ((image % 4 * 2 + half - z) * step + NZ) % NZ
            same = jnp.where(ahead <= 4, ahead, 20 - ahead)
            cross = jnp.where(ahead == 0, 8, jnp.where(ahead <= 3, 4 + ahead, 16 - ahead))
            for core in range(2):
                spot = jnp.where(c == core, same, cross)
                index = half * 2 + core
                source = rows_ref.at[k, pl.ds(index * ROWS, ROWS)]
                moves.append((spot, dh, source, sem.at[k, index]))
                move(moves[-1], mine_ref, other_ref, True)
    for one in moves:
        move(one, mine_ref, other_ref, False)


def move(one, mine_ref, other_ref, start):
    spot, dh, source, sem = one

    @pl.when(spot < 8)
    def _():
        copy = pltpu.make_async_copy(source, mine_ref.at[spot, dh], sem)
        copy.start() if start else copy.wait()

    @pl.when(spot >= 8)
    def _():
        copy = pltpu.make_async_copy(source, other_ref.at[spot - 8, dh], sem)
        copy.start() if start else copy.wait()


def early_kernel(*refs):
    sort_rows(refs[:4], OFFSETS[:4], *refs[4:])


def late_kernel(*refs):
    sort_rows(refs[2:6], OFFSETS[4:], *refs[6:])


def out_weights_kernel(*refs):
    acts, (all_ref, attn_ref, mlp_ref, acc_ref) = refs[:8], refs[8:]
    for k, (offset, act) in enumerate(zip(OFFSETS, acts)):
        start = pl.multiple_of(image_of(offset) * PATCH, PATCH)
        term = dot(act[...], all_ref[pl.ds(start, PATCH), :], 0, 0)
        if k == 0:
            acc_ref[...] = term
        else:
            acc_ref[...] += term
    attn_ref[...] = acc_ref[0:HD].astype(BF)
    mlp_ref[...] = acc_ref[HD:].astype(BF)


def in_early_kernel(*refs):
    grads, (all_ref, acc_ref) = refs[:4], refs[4:]
    for k, (offset, grad) in enumerate(zip(OFFSETS[:4], grads)):
        start = pl.multiple_of(image_of(offset) * PATCH, PATCH)
        term = dot(all_ref[pl.ds(start, PATCH), :], grad[...], 0, 0)
        if k == 0:
            acc_ref[...] = term
        else:
            acc_ref[...] += term


def in_late_kernel(*refs):
    grads, (all_ref, half_ref, w_qkv_ref, w_mlp_ref, qkv_ref, mlp_ref, gain_ref, acc_ref) = (
        refs[:4],
        refs[4:],
    )
    for k, (offset, grad) in enumerate(zip(OFFSETS[4:], grads)):
        start = pl.multiple_of(image_of(offset) * PATCH, PATCH)
        term = dot(all_ref[pl.ds(start, PATCH), :], grad[...], 0, 0)
        if k == 0:
            acc_ref[...] = half_ref[...] + term
        else:
            acc_ref[...] += term
    qkv = acc_ref[:, 0 : 3 * HD]
    mlp = acc_ref[:, 3 * HD :]
    qkv_ref[...] = qkv.astype(BF)
    mlp_ref[...] = mlp.astype(BF)
    gain_ref[...] = jnp.sum(qkv * w_qkv_ref[...].astype(F32), axis=1, keepdims=True) + jnp.sum(
        mlp * w_mlp_ref[...].astype(F32), axis=1, keepdims=True
    )


def add(*terms):
    total = terms[0].astype(F32)
    for term in terms[1:]:
        total = total + term.astype(F32)
    return total.astype(BF)


def gather_dp_first(own):
    return dp_send(own, Y_UP), dp_send(own, Y_DOWN), dp_send(own, X_SWAP)


def gather_dp_second(below, above, beside):
    return dp_send(beside, Y_DOWN), dp_send(beside, Y_UP)


def gather_dp_third(own, below, above, beside, beside_above, beside_below):
    far = dp_send(below, Y_UP)
    beside_far = dp_send(beside_above, Y_DOWN)
    return [own, above, below, beside, far, beside_above, beside_below, beside_far]


def scatter_dp(parts):
    own, above, below, beside, far, beside_above, beside_below, beside_far = parts
    down = dp_send(far, Y_DOWN)
    up = dp_send(beside_far, Y_UP)
    down_beside = dp_send(beside_below, Y_DOWN)
    up_beside = dp_send(add(beside_above, up), Y_UP)
    down_last = dp_send(add(below, down), Y_DOWN)
    up_last = dp_send(above, Y_UP)
    across = dp_send(add(beside, down_beside, up_beside), X_SWAP)
    return own, down_last, up_last, across


def gather_mp(own, act, scaled):
    own_pair = jnp.stack([own, mp_send(own, H_SWAP)])
    own_pair, act = lax.optimization_barrier((own_pair, act))
    first = gather_dp_first(act)
    other_pair = mp_send(own_pair, C_SWAP)
    mine_a, mine_b = [mp_send(own_pair, Z_RING)], [mp_send(other_pair, Z_RING)]
    mine_a.append(mp_send(mine_a[-1], Z_RING))
    mine_a, mine_b, first = lax.optimization_barrier((mine_a, mine_b, first))
    second = gather_dp_second(*first)
    mine_a.append(mp_send(mine_a[-1], Z_RING))
    mine_b.append(mp_send(mine_b[-1], Z_RING))
    mine_a, mine_b, second, scaled = lax.optimization_barrier((mine_a, mine_b, second, scaled))
    all_acts = gather_dp_third(act, *first, *second)
    mine_a.append(mp_send(mine_a[-1], Z_RING))
    mine_b.append(mp_send(mine_b[-1], Z_RING))
    mine = jnp.stack(mine_a[:3] + mine_b)
    last, all_acts = lax.optimization_barrier((mine_a[3], all_acts))
    theirs, theirs_last = mp_send(mine, C_SWAP), mp_send(last, C_SWAP)
    return [own_pair, other_pair, mine, last, theirs, theirs_last], all_acts, scaled


def scatter_mp(mine, other, tied):
    held = add(mine, mp_send(other, C_SWAP))
    ring_a = mp_send(held[4], Z_RING)
    ring_b = mp_send(held[7], Z_RING)
    ring_a = mp_send(add(held[3], ring_a), Z_RING)
    ring_b = mp_send(add(held[6], ring_b), Z_RING)
    ring_a, tied = lax.optimization_barrier((ring_a, tied))
    gain = tied[2]
    ring_a = mp_send(add(held[2], ring_a), Z_RING)
    ring_b = mp_send(add(held[5], ring_b), Z_RING)
    gain = gain + mp_send(gain, C_SWAP)
    ring_a, gain = lax.optimization_barrier((ring_a, gain))
    ring_a = mp_send(add(held[1], ring_a), Z_RING)
    ring_b = mp_send(ring_b, C_SWAP)
    gain = gain + mp_send(gain, H_SWAP)
    ring_a, gain = lax.optimization_barrier((ring_a, gain))
    across = mp_send(add(held[0, 1], ring_a[1], ring_b[1]), H_SWAP)
    gain = gain + mp_send(gain, Z_XOR[0])
    across, gain = lax.optimization_barrier((across, gain))
    total = across.astype(F32)
    for term in (held[0, 0], ring_a[0], ring_b[0]):
        total = total + term.astype(F32)
    return total, tied[:2], gain


def sum_all(values, gain):
    values = values + dp_send(values, X_SWAP)
    gain = gain + mp_send(gain, Z_XOR[1])
    values, gain = lax.optimization_barrier((values, gain))
    others = [dp_send(values, perm) for perm in (Y_UP, Y_DOWN, Y_TWO)]
    gain = gain + mp_send(gain, Z_XOR[2])
    return values + others[0] + others[1] + others[2], gain


def per_device(
    block_input, ln_gain, qkv_act, mlp_pre, out_grad, w_qkv, w_mlp, w_out_attn, w_out_mlp
):
    width = block_input.shape[1]
    shape = jax.ShapeDtypeStruct
    widened = block_input.astype(F32)
    mean = jnp.mean(widened, axis=1)
    square = jnp.sum(jnp.square(widened - mean[:, None]), axis=1)
    count = width
    for perm in (X_SWAP, Y_ONE, Y_TWO):
        theirs = dp_send(jnp.stack([mean, square]), perm)
        gap = mean - theirs[0]
        square = square + theirs[1] + gap * gap * (count / 2)
        mean = (mean + theirs[0]) * 0.5
        count = count * 2
    inverse = lax.rsqrt(square / D + eps)
    normed = (widened - mean[:, None]) * inverse[:, None]
    scaled = (normed * ln_gain[None, :]).astype(BF)
    act = call(
        forward_kernel, shape((PATCH, 896), BF), 2, 10, flops=10**8, nbytes=2 * 10**6
    )(qkv_act, mlp_pre)
    pieces, all_acts, scaled = gather_mp(out_grad, act, scaled)
    all_scaled = lax.all_gather(scaled, "mp", axis=0, tiled=True)
    pieces, all_acts = lax.optimization_barrier((pieces, all_acts))
    part_shape = [shape((PATCH, 896), BF)] * 4
    all_grad, *first = call(
        spread_kernel,
        [shape((2048, 768), BF)] + part_shape,
        8,
        16,
        flops=2048 * 768 * 896,
        nbytes=10 * 10**6,
    )(*pieces, w_out_attn, w_out_mlp)
    second = call(parts_kernel, part_shape, 3, 14, flops=2048 * 768 * 896, nbytes=6 * 10**6)(
        all_grad, w_out_attn, w_out_mlp
    )
    parts = [None] * 8
    for index, part in zip(FIRST + SECOND, first + list(second)):
        parts[index] = part
    sums = scatter_dp(parts)
    grad = call(
        middle_kernel, shape((PATCH, 1152), BF), 6, 14, flops=2 * 10**8, nbytes=3 * 10**6
    )(qkv_act, mlp_pre, *sums)
    near = gather_dp_first(grad)
    acc_attn, acc_mlp = call(
        out_weights_kernel,
        [shape((HD, 768), BF), shape((768, 768), BF)],
        9,
        22,
        scratch=[pltpu.VMEM((896, 768), F32)],
        flops=2 * 2048 * 768 * 896,
        nbytes=8 * 10**6,
    )(*all_acts, all_grad)
    near, all_scaled, acc_attn, acc_mlp = lax.optimization_barrier(
        (near, all_scaled, acc_attn, acc_mlp)
    )
    grads = gather_dp_third(grad, *near, *gather_dp_second(*near))
    early, late = grads[:4], grads[4:]
    slots = [shape((8, NH, ROWS, 768), BF)] * 2
    sort_scratch = [pltpu.VMEM((4, PATCH, 768), BF), pltpu.SemaphoreType.DMA((4, 4))]
    mine, other = call(
        early_kernel,
        slots,
        6,
        16,
        flops=2048 * 768 * 1152,
        nbytes=6 * 10**6,
        scratch=sort_scratch,
        any_out=True,
    )(*early, w_qkv, w_mlp)
    acc_half = call(
        in_early_kernel,
        shape((768, 1152), F32),
        5,
        18,
        flops=2048 * 768 * 1152,
        nbytes=9 * 10**6,
    )(*early, all_scaled)
    late, acc_half = lax.optimization_barrier((late, acc_half))
    mine, other = call(
        late_kernel,
        slots,
        8,
        16,
        flops=2048 * 768 * 1152,
        nbytes=6 * 10**6,
        scratch=sort_scratch,
        any_in=(0, 1),
        any_out=True,
        aliases={0: 0, 1: 1},
    )(mine, other, *late, w_qkv, w_mlp)
    acc_qkv, acc_pre, gain_part = call(
        in_late_kernel,
        [shape((768, 384), BF), shape((768, 768), BF), shape((768, 1), F32)],
        8,
        24,
        scratch=[pltpu.VMEM((768, 1152), F32)],
        flops=2048 * 768 * 1152,
        nbytes=12 * 10**6,
    )(*late, all_scaled, acc_half, w_qkv, w_mlp)
    grad_normed, (acc_qkv, acc_pre), gain_grad = scatter_mp(
        mine, other, (acc_qkv, acc_pre, gain_part[:, 0] / ln_gain)
    )
    weighted = grad_normed * ln_gain[None, :]
    sums = jnp.stack([jnp.sum(weighted, axis=1), jnp.sum(weighted * normed, axis=1)])
    sums, gain_grad = sum_all(sums, gain_grad)
    sums = sums / D
    input_grad = out_grad.astype(F32) + inverse[:, None] * (
        weighted - sums[0][:, None] - normed * sums[1][:, None]
    )
    return (input_grad.astype(BF), acc_qkv, acc_pre, acc_attn, acc_mlp, gain_grad)


def solution(mesh):
    return jax.shard_map(
        per_device,
        mesh=mesh,
        in_specs=(
            P("mp", "dp"),
            P("dp"),
            P("dp", "mp"),
            P("dp", "mp"),
            P("mp", "dp"),
            P("dp", "mp"),
            P("dp", "mp"),
            P("mp", "dp"),
            P("mp", "dp"),
        ),
        out_specs=(
            P("mp", "dp"),
            P("dp", "mp"),
            P("dp", "mp"),
            P("mp", "dp"),
            P("mp", "dp"),
            P("dp"),
        ),
        check_vma=False,
    )
```

```python
import jax
import jax.numpy as jnp
from jax import lax
from jax.experimental import pallas as pl
from jax.experimental.pallas import tpu as pltpu
from jax.sharding import PartitionSpec as P

D = 6144
HD = 128
PATCH = 256
eps = 1e-06
BF = jnp.bfloat16
F32 = jnp.float32

NY, NX, NH, NZ, NC = 4, 2, 2, 8, 2
ROWS = 64


def dp_perm(move):
    pairs = []
    for y in range(NY):
        for x in range(NX):
            to_y, to_x = move(y, x)
            pairs.append((y * NX + x, (to_y % NY) * NX + to_x))
    return pairs


def mp_perm(move):
    pairs = []
    for h in range(NH):
        for z in range(NZ):
            for c in range(NC):
                to_h, to_z, to_c = move(h, z, c)
                pairs.append(((h * NZ + z) * NC + c, (to_h * NZ + to_z % NZ) * NC + to_c))
    return pairs


X_SWAP = dp_perm(lambda y, x: (y, 1 - x))
Y_UP = dp_perm(lambda y, x: (y + 1, x))
Y_DOWN = dp_perm(lambda y, x: (y - 1, x))
Y_TWO = dp_perm(lambda y, x: (y ^ 2, x))
H_SWAP = mp_perm(lambda h, z, c: (1 - h, z, c))
C_SWAP = mp_perm(lambda h, z, c: (h, z, 1 - c))
Z_RING = mp_perm(lambda h, z, c: (h, z + 1 - 2 * c, c))

OFFSETS = [(0, 0), (1, 0), (3, 0), (0, 1), (2, 0), (1, 1), (3, 1), (2, 1)]


def dp_send(array, perm):
    return lax.ppermute(array, "dp", perm)


def mp_send(array, perm):
    return lax.ppermute(array, "mp", perm)


def dp_place():
    index = lax.axis_index("dp")
    return index // NX, index % NX


def mp_place():
    index = lax.axis_index("mp")
    return index // (NZ * NC), (index // NC) % NZ, index % NC


def image_of(offset):
    y, x = dp_place()
    dy, dx = offset
    return ((y + dy) % NY) * NX + (x + dx) % NX


def dot(a, b, ca, cb):
    return lax.dot_general(a, b, (((ca,), (cb,)), ((), ())), preferred_element_type=F32)


def call(kernel, out_shape, n_in, limit, flops=0, nbytes=0):
    return pl.pallas_call(
        kernel,
        out_shape=out_shape,
        in_specs=[pl.BlockSpec(memory_space=pltpu.VMEM)] * n_in,
        out_specs=jax.tree.map(lambda _: pl.BlockSpec(memory_space=pltpu.VMEM), out_shape),
        compiler_params=pltpu.CompilerParams(vmem_limit_bytes=limit * 1024 * 1024),
        cost_estimate=pl.CostEstimate(flops=flops, bytes_accessed=nbytes, transcendentals=0),
    )


def staged_call(
    kernel, out_shape, args, limit, flops, nbytes, scratch=(), held=0, any_out=False, staged=True
):
    moved = args[held:] if staged else []

    def body(*refs):
        sources, rest = refs[held : len(args)], refs[len(args) :]
        outs, rest = rest[: len(out_shape)], rest[len(out_shape) :]
        own, buffers = rest[: len(scratch)], rest[len(scratch) : len(scratch) + len(moved)]
        if not staged:
            kernel(lambda i: sources[i], outs, own)
            return
        sem = rest[-1]
        copies = [
            pltpu.make_async_copy(source, buffer, sem.at[i])
            for i, (source, buffer) in enumerate(zip(sources, buffers))
        ]
        for copy in copies:
            copy.start()

        def take(i):
            copies[i].wait()
            return buffers[i]

        kernel(take, outs, own)

    return pl.pallas_call(
        body,
        out_shape=out_shape,
        in_specs=[pl.BlockSpec(memory_space=pl.ANY)] * held
        + [pl.BlockSpec(memory_space=pl.ANY if staged else pltpu.VMEM)] * (len(args) - held),
        out_specs=[pl.BlockSpec(memory_space=pl.ANY if any_out else pltpu.VMEM)] * len(out_shape),
        scratch_shapes=list(scratch)
        + [pltpu.VMEM(one.shape, one.dtype) for one in moved]
        + [pltpu.SemaphoreType.DMA((len(moved),))] * staged,
        input_output_aliases={i: i for i in range(held)},
        compiler_params=pltpu.CompilerParams(vmem_limit_bytes=limit * 1024 * 1024),
        cost_estimate=pl.CostEstimate(flops=flops, bytes_accessed=nbytes, transcendentals=0),
    )(*args)


GELU_C = 0.7978845608028654
GELU_A = 0.044715


def attn_probs_of(query, key):
    scores = dot(query, key, 1, 1) * (HD**-0.5)
    scores = scores - jnp.max(scores, axis=-1, keepdims=True)
    powers = jnp.exp(scores)
    return powers / jnp.sum(powers, axis=-1, keepdims=True)


def forward_kernel(qkv_ref, pre_ref, act_ref):
    probs = attn_probs_of(qkv_ref[:, 0:HD], qkv_ref[:, HD : 2 * HD])
    attended = dot(probs.astype(BF), qkv_ref[:, 2 * HD : 3 * HD], 1, 0)
    act_ref[:, 0:HD] = attended.astype(BF)
    pre = pre_ref[...].astype(F32)
    inner = jnp.tanh(GELU_C * (pre + GELU_A * pre * pre * pre))
    act_ref[:, HD:] = (0.5 * pre * (1.0 + inner)).astype(BF)


def part_of(offset, all_ref, w_attn_ref, w_mlp_ref, part):
    start = pl.multiple_of(image_of(offset) * PATCH, PATCH)
    rows = all_ref[pl.ds(start, PATCH), :]
    part[:, 0:HD] = dot(rows, w_attn_ref[...], 1, 1).astype(BF)
    part[:, HD:] = dot(rows, w_mlp_ref[...], 1, 1).astype(BF)


FIRST = [4, 7, 6, 1]
SECOND = [5, 2, 3, 0]


def spread_kernel(*refs):
    pieces, (w_attn_ref, w_mlp_ref, all_ref), parts = refs[:6], refs[6:9], refs[9:]
    own_pair, other_pair, mine, last, theirs, theirs_last = pieces
    h, z, c = mp_place()
    step = 1 - 2 * c

    def put(piece, place_z, core):
        for dh in range(NH):
            spot = ((h + dh) % NH * NZ + (place_z + 2 * NZ) % NZ) * NC + core
            all_ref[pl.ds(pl.multiple_of(spot * ROWS, ROWS), ROWS), :] = piece[dh]

    put(own_pair, z, c)
    put(other_pair, z, 1 - c)
    put(last, z - step * 4, c)
    put(theirs_last, z + step * 4, 1 - c)
    for r in range(1, 4):
        put(mine.at[r - 1], z - step * r, c)
        put(theirs.at[r - 1], z + step * r, 1 - c)
        put(mine.at[r + 2], z - step * r, 1 - c)
        put(theirs.at[r + 2], z + step * r, c)
    for index, part in zip(FIRST, parts):
        part_of(OFFSETS[index], all_ref, w_attn_ref, w_mlp_ref, part)


def parts_kernel(all_ref, w_attn_ref, w_mlp_ref, *parts):
    for index, part in zip(SECOND, parts):
        part_of(OFFSETS[index], all_ref, w_attn_ref, w_mlp_ref, part)


def middle_kernel(qkv_ref, pre_ref, a_ref, b_ref, c_ref, d_ref, grad_ref):
    total = (
        a_ref[...].astype(F32)
        + b_ref[...].astype(F32)
        + c_ref[...].astype(F32)
        + d_ref[...].astype(F32)
    )
    upward = total[:, 0:HD].astype(BF)
    query, key, value = (qkv_ref[:, i * HD : (i + 1) * HD] for i in range(3))
    probs = attn_probs_of(query, key)
    rounded = probs.astype(BF)
    grad_value = dot(rounded, upward, 0, 0)
    grad_probs = dot(upward, value, 1, 1)
    centred = grad_probs - jnp.sum(grad_probs * probs, axis=-1, keepdims=True)
    grad_scores = (probs * centred * (HD**-0.5)).astype(BF)
    grad_ref[:, 0:HD] = dot(grad_scores, key, 1, 0).astype(BF)
    grad_ref[:, HD : 2 * HD] = dot(grad_scores, query, 0, 0).astype(BF)
    grad_ref[:, 2 * HD : 3 * HD] = grad_value.astype(BF)
    pre = pre_ref[...].astype(F32)
    inner = jnp.tanh(GELU_C * (pre + GELU_A * pre * pre * pre))
    slope = 0.5 * (1.0 + inner) + 0.5 * pre * (1.0 - inner * inner) * (
        GELU_C * (1.0 + 3.0 * GELU_A * pre * pre)
    )
    grad_ref[:, 3 * HD :] = (total[:, HD:] * slope).astype(BF)


def sort_rows(take, offsets, mine_ref, other_ref, rows_ref, sem):
    h, z, c = mp_place()
    step = 1 - 2 * c
    w_qkv_ref, w_mlp_ref = take(0), take(1)
    moves = []
    for k, offset in enumerate(offsets):
        grad = take(k + 2)
        image = image_of(offset)
        rows = dot(grad[:, 0 : 3 * HD], w_qkv_ref[...], 1, 1) + dot(
            grad[:, 3 * HD :], w_mlp_ref[...], 1, 1
        )
        rows_ref[k] = rows.astype(BF)
        dh = (image // 4 + h) % NH
        for half in range(2):
            ahead = ((image % 4 * 2 + half - z) * step + NZ) % NZ
            same = jnp.where(ahead <= 4, ahead, 20 - ahead)
            cross = jnp.where(ahead == 0, 8, jnp.where(ahead <= 3, 4 + ahead, 16 - ahead))
            for core in range(2):
                spot = jnp.where(c == core, same, cross)
                index = half * 2 + core
                source = rows_ref.at[k, pl.ds(index * ROWS, ROWS)]
                moves.append((spot, dh, source, sem.at[k, index]))
                move(moves[-1], mine_ref, other_ref, True)
    for one in moves:
        move(one, mine_ref, other_ref, False)


def move(one, mine_ref, other_ref, start):
    spot, dh, source, sem = one

    @pl.when(spot < 8)
    def _():
        copy = pltpu.make_async_copy(source, mine_ref.at[spot, dh], sem)
        copy.start() if start else copy.wait()

    @pl.when(spot >= 8)
    def _():
        copy = pltpu.make_async_copy(source, other_ref.at[spot - 8, dh], sem)
        copy.start() if start else copy.wait()


def early_kernel(take, outs, own):
    sort_rows(take, OFFSETS[:4], *outs, *own)


def late_kernel(take, outs, own):
    sort_rows(take, OFFSETS[4:], *outs, *own)


def out_weights_kernel(take, outs, own):
    (attn_ref, mlp_ref), (acc_ref,) = outs, own
    all_ref = take(0)
    for k, offset in enumerate(OFFSETS):
        start = pl.multiple_of(image_of(offset) * PATCH, PATCH)
        term = dot(take(k + 1)[...], all_ref[pl.ds(start, PATCH), :], 0, 0)
        if k == 0:
            acc_ref[...] = term
        else:
            acc_ref[...] += term
    attn_ref[...] = acc_ref[0:HD].astype(BF)
    mlp_ref[...] = acc_ref[HD:].astype(BF)


def in_weights_kernel(take, outs, own):
    (qkv_ref, mlp_ref, gain_ref), (acc_ref,) = outs, own
    all_ref = take(0)
    for k, offset in enumerate(OFFSETS):
        start = pl.multiple_of(image_of(offset) * PATCH, PATCH)
        term = dot(all_ref[pl.ds(start, PATCH), :], take(k + 1)[...], 0, 0)
        if k == 0:
            acc_ref[...] = term
        else:
            acc_ref[...] += term
    qkv = acc_ref[:, 0 : 3 * HD]
    mlp = acc_ref[:, 3 * HD :]
    qkv_ref[...] = qkv.astype(BF)
    mlp_ref[...] = mlp.astype(BF)
    total = 0.0
    for product in (qkv * take(9)[...].astype(F32), mlp * take(10)[...].astype(F32)):
        total = total + lax.dot_general(
            jnp.ones((8, product.shape[1]), F32),
            product,
            (((1,), (1,)), ((), ())),
            precision=lax.Precision.HIGHEST,
            preferred_element_type=F32,
        )
    gain_ref[...] = total


def add(*terms):
    total = terms[0].astype(F32)
    for term in terms[1:]:
        total = total + term.astype(F32)
    return total.astype(BF)


def gather_dp_first(own):
    return dp_send(own, Y_UP), dp_send(own, Y_DOWN), dp_send(own, X_SWAP)


def gather_dp_second(below, above, beside):
    return dp_send(beside, Y_DOWN), dp_send(beside, Y_UP)


def gather_dp_third(own, below, above, beside, beside_above, beside_below):
    far = dp_send(below, Y_UP)
    beside_far = dp_send(beside_above, Y_DOWN)
    return [own, above, below, beside, far, beside_above, beside_below, beside_far]


def scatter_dp(parts):
    own, above, below, beside, far, beside_above, beside_below, beside_far = parts
    down = dp_send(far, Y_DOWN)
    up = dp_send(beside_far, Y_UP)
    down_beside = dp_send(beside_below, Y_DOWN)
    up_beside = dp_send(add(beside_above, up), Y_UP)
    down_last = dp_send(add(below, down), Y_DOWN)
    up_last = dp_send(above, Y_UP)
    across = dp_send(add(beside, down_beside, up_beside), X_SWAP)
    return own, down_last, up_last, across


def join_stats(mean, square, count, theirs):
    means = [mean] + [one[0] for one in theirs]
    squares = [square] + [one[1] for one in theirs]
    joined = sum(means) / len(means)
    spread = sum(jnp.square(one - joined) for one in means)
    return joined, sum(squares) + count * spread


def gather_mp(own, act, widened):
    width = widened.shape[1]
    mean = jnp.mean(widened, axis=1)
    square = jnp.sum(jnp.square(widened - mean[:, None]), axis=1)
    theirs = dp_send(jnp.stack([mean, square]), X_SWAP)
    own_pair = jnp.stack([own, mp_send(own, H_SWAP)])
    own_pair, theirs, act = lax.optimization_barrier((own_pair, theirs, act))
    mean, square = join_stats(mean, square, width, [theirs])
    stats = jnp.stack([mean, square])
    theirs = [dp_send(stats, perm) for perm in (Y_UP, Y_DOWN, Y_TWO)]
    other_pair = mp_send(own_pair, C_SWAP)
    mine_a = [mp_send(own_pair, Z_RING)]
    mine_a, other_pair, theirs, act = lax.optimization_barrier((mine_a, other_pair, theirs, act))
    stats = join_stats(mean, square, 2 * width, theirs)
    first = gather_dp_first(act)
    mine_b = [mp_send(other_pair, Z_RING)]
    mine_a.append(mp_send(mine_a[-1], Z_RING))
    mine_a.append(mp_send(mine_a[-1], Z_RING))
    mine_b.append(mp_send(mine_b[-1], Z_RING))
    mine_a, mine_b, first = lax.optimization_barrier((mine_a, mine_b, first))
    second = gather_dp_second(*first)
    mine_a.append(mp_send(mine_a[-1], Z_RING))
    mine_b.append(mp_send(mine_b[-1], Z_RING))
    mine = jnp.stack(mine_a[:3] + mine_b)
    last, second = lax.optimization_barrier((mine_a[3], second))
    theirs, theirs_last = mp_send(mine, C_SWAP), mp_send(last, C_SWAP)
    pieces = [own_pair, other_pair, mine, last, theirs, theirs_last]
    return pieces, gather_dp_third(act, *first, *second), stats


def pack(value):
    high = lax.reduce_precision(value, 8, 7)
    middle = lax.reduce_precision(value - high, 8, 7)
    rows = jnp.stack([high, middle, value - high - middle]).astype(BF)
    return jnp.pad(rows, ((0, 13), (0, 0)))


def unpack(rows):
    rows = rows.astype(F32)
    return rows[0] + rows[1] + rows[2]


def with_rows(block, *rows):
    return jnp.concatenate([block.reshape(-1, block.shape[-1]), *rows])


def scatter_mp(mine, other, gain, acts, finish):
    height = 2 * ROWS
    received = mp_send(other, C_SWAP)
    gain = gain + mp_send(gain, C_SWAP)
    received, gain = lax.optimization_barrier((received, gain))
    held = add(mine, received)
    got = mp_send(with_rows(held[4], pack(gain)), Z_RING)
    ring_b = mp_send(held[7], Z_RING)
    passed = []
    for step in range(3):
        rows = got[height:]
        passed.append(rows)
        block = add(held[3 - step].reshape(height, -1), got[:height])
        got = mp_send(with_rows(block, rows), Z_RING)
        if step < 2:
            ring_b = mp_send(add(held[6 - step], ring_b), Z_RING)
            if step == 1:
                got, acts = lax.optimization_barrier((got, acts))
        else:
            ring_b = mp_send(with_rows(ring_b, *passed), C_SWAP)
    got, tied = lax.optimization_barrier((got, finish(acts)))
    ring_a = got[:height].reshape(NH, ROWS, -1)
    opposite = ring_b[height:]
    ring_b = ring_b[:height].reshape(NH, ROWS, -1)
    _, z, c = mp_place()
    step = 1 - 2 * c
    sums = [(z, gain), (z + 4, unpack(got[height:]))]
    for r in range(3):
        sums.append((z - step * (r + 1), unpack(passed[r])))
        sums.append((z + step * (r + 1), unpack(opposite[16 * r : 16 * r + 16])))
    spots = jnp.arange(NZ)[:, None]
    ordered = sum(jnp.where(spots == (at + NZ) % NZ, one[None, :], 0.0) for at, one in sums)
    gain = ordered[0]
    for index in range(1, NZ):
        gain = gain + ordered[index]
    across = mp_send(
        with_rows(add(held[0, 1], ring_a[1], ring_b[1]), pack(gain)), H_SWAP
    )
    total = across[:ROWS].astype(F32)
    for term in (held[0, 0], ring_a[0], ring_b[0]):
        total = total + term.astype(F32)
    gain = unpack(pack(gain)) + unpack(across[ROWS:])
    return total, tied, gain


def sum_dp(values):
    values = values + dp_send(values, X_SWAP)
    others = [dp_send(values, perm) for perm in (Y_UP, Y_DOWN, Y_TWO)]
    return values + others[0] + others[1] + others[2]


def per_device(
    block_input, ln_gain, qkv_act, mlp_pre, out_grad, w_qkv, w_mlp, w_out_attn, w_out_mlp
):
    shape = jax.ShapeDtypeStruct
    widened = block_input.astype(F32)
    act = call(
        forward_kernel, shape((PATCH, 896), BF), 2, 10, flops=10**8, nbytes=2 * 10**6
    )(qkv_act, mlp_pre)
    pieces, all_acts, (mean, square) = gather_mp(out_grad, act, widened)
    inverse = lax.rsqrt(square / D + eps)
    normed = (widened - mean[:, None]) * inverse[:, None]
    scaled = (normed * ln_gain[None, :]).astype(BF)
    all_scaled = lax.all_gather(scaled, "mp", axis=0, tiled=True)
    part_shape = [shape((PATCH, 896), BF)] * 4
    all_grad, *first = call(
        spread_kernel,
        [shape((2048, 768), BF)] + part_shape,
        8,
        16,
        flops=2048 * 768 * 896,
        nbytes=10 * 10**6,
    )(*pieces, w_out_attn, w_out_mlp)
    second = call(parts_kernel, part_shape, 3, 14, flops=2048 * 768 * 896, nbytes=6 * 10**6)(
        all_grad, w_out_attn, w_out_mlp
    )
    parts = [None] * 8
    for index, part in zip(FIRST + SECOND, first + list(second)):
        parts[index] = part
    sums = scatter_dp(parts)
    grad = call(
        middle_kernel, shape((PATCH, 1152), BF), 6, 14, flops=2 * 10**8, nbytes=3 * 10**6
    )(qkv_act, mlp_pre, *sums)
    near = gather_dp_first(grad)
    near, all_scaled = lax.optimization_barrier((near, all_scaled))
    grads = gather_dp_third(grad, *near, *gather_dp_second(*near))
    early, late = grads[:4], grads[4:]
    slots = [shape((8, NH, ROWS, 768), BF)] * 2
    sort_scratch = [pltpu.VMEM((4, PATCH, 768), BF), pltpu.SemaphoreType.DMA((4, 4))]
    mine, other = staged_call(
        early_kernel,
        slots,
        [w_qkv, w_mlp, *early],
        16,
        2048 * 768 * 1152,
        6 * 10**6,
        scratch=sort_scratch,
        staged=False,
        any_out=True,
    )
    late, mine = lax.optimization_barrier((late, mine))
    mine, other = staged_call(
        late_kernel,
        slots,
        [mine, other, w_qkv, w_mlp, *late],
        16,
        2048 * 768 * 1152,
        6 * 10**6,
        scratch=sort_scratch,
        staged=False,
        held=2,
        any_out=True,
    )
    acc_qkv, acc_pre, gain_part = staged_call(
        in_weights_kernel,
        [shape((768, 384), BF), shape((768, 768), BF), shape((8, 768), F32)],
        [all_scaled, *early, *late, w_qkv, w_mlp],
        60,
        2 * 2048 * 768 * 1152,
        12 * 10**6,
        scratch=[pltpu.VMEM((768, 1152), F32)],
    )

    def finish(acts):
        return staged_call(
            out_weights_kernel,
            [shape((HD, 768), BF), shape((768, 768), BF)],
            [all_grad, *acts],
            60,
            2 * 2048 * 768 * 896,
            8 * 10**6,
            scratch=[pltpu.VMEM((896, 768), F32)],
        )

    grad_normed, (acc_attn, acc_mlp), gain_grad = scatter_mp(
        mine, other, gain_part[0] / ln_gain, all_acts, finish
    )
    weighted = grad_normed * ln_gain[None, :]
    sums = jnp.stack([jnp.sum(weighted, axis=1), jnp.sum(weighted * normed, axis=1)])
    sums = sum_dp(sums) / D
    input_grad = out_grad.astype(F32) + inverse[:, None] * (
        weighted - sums[0][:, None] - normed * sums[1][:, None]
    )
    return (input_grad.astype(BF), acc_qkv, acc_pre, acc_attn, acc_mlp, gain_grad)


def solution(mesh):
    return jax.shard_map(
        per_device,
        mesh=mesh,
        in_specs=(
            P("mp", "dp"),
            P("dp"),
            P("dp", "mp"),
            P("dp", "mp"),
            P("mp", "dp"),
            P("dp", "mp"),
            P("dp", "mp"),
            P("mp", "dp"),
            P("mp", "dp"),
        ),
        out_specs=(
            P("mp", "dp"),
            P("dp", "mp"),
            P("dp", "mp"),
            P("mp", "dp"),
            P("mp", "dp"),
            P("dp"),
        ),
        check_vma=False,
    )
```

```python
import jax
import jax.numpy as jnp
from jax import lax
from jax.experimental import pallas as pl
from jax.experimental.pallas import tpu as pltpu
from jax.sharding import PartitionSpec as P

D = 6144
HD = 128
PATCH = 256
eps = 1e-06
BF = jnp.bfloat16
F32 = jnp.float32

NY, NX, NH, NZ, NC = 4, 2, 2, 8, 2
ROWS = 64


def dp_perm(move):
    pairs = []
    for y in range(NY):
        for x in range(NX):
            to_y, to_x = move(y, x)
            pairs.append((y * NX + x, (to_y % NY) * NX + to_x))
    return pairs


def mp_perm(move):
    pairs = []
    for h in range(NH):
        for z in range(NZ):
            for c in range(NC):
                to_h, to_z, to_c = move(h, z, c)
                pairs.append(((h * NZ + z) * NC + c, (to_h * NZ + to_z % NZ) * NC + to_c))
    return pairs


X_SWAP = dp_perm(lambda y, x: (y, 1 - x))
Y_UP = dp_perm(lambda y, x: (y + 1, x))
Y_DOWN = dp_perm(lambda y, x: (y - 1, x))
Y_TWO = dp_perm(lambda y, x: (y ^ 2, x))
H_SWAP = mp_perm(lambda h, z, c: (1 - h, z, c))
C_SWAP = mp_perm(lambda h, z, c: (h, z, 1 - c))
Z_RING = mp_perm(lambda h, z, c: (h, z + 1 - 2 * c, c))

OFFSETS = [(0, 0), (1, 0), (3, 0), (0, 1), (2, 0), (1, 1), (3, 1), (2, 1)]


def dp_send(array, perm):
    return lax.ppermute(array, "dp", perm)


def mp_send(array, perm):
    return lax.ppermute(array, "mp", perm)


def dp_place():
    index = lax.axis_index("dp")
    return index // NX, index % NX


def mp_place():
    index = lax.axis_index("mp")
    return index // (NZ * NC), (index // NC) % NZ, index % NC


def image_of(offset):
    y, x = dp_place()
    dy, dx = offset
    return ((y + dy) % NY) * NX + (x + dx) % NX


def dot(a, b, ca, cb):
    return lax.dot_general(a, b, (((ca,), (cb,)), ((), ())), preferred_element_type=F32)


def call(kernel, out_shape, n_in, limit, flops=0, nbytes=0):
    return pl.pallas_call(
        kernel,
        out_shape=out_shape,
        in_specs=[pl.BlockSpec(memory_space=pltpu.VMEM)] * n_in,
        out_specs=jax.tree.map(lambda _: pl.BlockSpec(memory_space=pltpu.VMEM), out_shape),
        compiler_params=pltpu.CompilerParams(vmem_limit_bytes=limit * 1024 * 1024),
        cost_estimate=pl.CostEstimate(flops=flops, bytes_accessed=nbytes, transcendentals=0),
    )


def staged_call(
    kernel, out_shape, args, limit, flops, nbytes, scratch=(), held=0, any_out=0, staged=True
):
    moved = args[held:] if staged else []

    def body(*refs):
        sources, rest = refs[held : len(args)], refs[len(args) :]
        outs, rest = rest[: len(out_shape)], rest[len(out_shape) :]
        own, buffers = rest[: len(scratch)], rest[len(scratch) : len(scratch) + len(moved)]
        if not staged:
            kernel(lambda i: sources[i], outs, own)
            return
        sem = rest[-1]
        copies = [
            pltpu.make_async_copy(source, buffer, sem.at[i])
            for i, (source, buffer) in enumerate(zip(sources, buffers))
        ]
        for copy in copies:
            copy.start()

        def take(i):
            copies[i].wait()
            return buffers[i]

        kernel(take, outs, own)

    return pl.pallas_call(
        body,
        out_shape=out_shape,
        in_specs=[pl.BlockSpec(memory_space=pl.ANY)] * held
        + [pl.BlockSpec(memory_space=pl.ANY if staged else pltpu.VMEM)] * (len(args) - held),
        out_specs=[
            pl.BlockSpec(memory_space=pl.ANY if i < any_out else pltpu.VMEM)
            for i in range(len(out_shape))
        ],
        scratch_shapes=list(scratch)
        + [pltpu.VMEM(one.shape, one.dtype) for one in moved]
        + [pltpu.SemaphoreType.DMA((len(moved),))] * staged,
        input_output_aliases={i: i for i in range(held)},
        compiler_params=pltpu.CompilerParams(vmem_limit_bytes=limit * 1024 * 1024),
        cost_estimate=pl.CostEstimate(flops=flops, bytes_accessed=nbytes, transcendentals=0),
    )(*args)


GELU_C = 0.7978845608028654
GELU_A = 0.044715


def attn_probs_of(query, key):
    scores = dot(query, key, 1, 1) * (HD**-0.5)
    scores = scores - jnp.max(scores, axis=-1, keepdims=True)
    powers = jnp.exp(scores)
    return powers / jnp.sum(powers, axis=-1, keepdims=True)


def forward_kernel(qkv_ref, pre_ref, act_ref):
    probs = attn_probs_of(qkv_ref[:, 0:HD], qkv_ref[:, HD : 2 * HD])
    attended = dot(probs.astype(BF), qkv_ref[:, 2 * HD : 3 * HD], 1, 0)
    act_ref[:, 0:HD] = attended.astype(BF)
    pre = pre_ref[...].astype(F32)
    inner = jnp.tanh(GELU_C * (pre + GELU_A * pre * pre * pre))
    act_ref[:, HD:] = (0.5 * pre * (1.0 + inner)).astype(BF)


def part_of(offset, all_ref, w_attn_ref, w_mlp_ref, part):
    start = pl.multiple_of(image_of(offset) * PATCH, PATCH)
    rows = all_ref[pl.ds(start, PATCH), :]
    part[:, 0:HD] = dot(rows, w_attn_ref[...], 1, 1).astype(BF)
    part[:, HD:] = dot(rows, w_mlp_ref[...], 1, 1).astype(BF)


FIRST = [4, 7, 6, 1]
SECOND = [5, 2, 3, 0]


def spread_kernel(*refs):
    pieces, (w_attn_ref, w_mlp_ref, all_ref), parts = refs[:6], refs[6:9], refs[9:]
    own_pair, other_pair, mine, last, theirs, theirs_last = pieces
    h, z, c = mp_place()
    step = 1 - 2 * c

    def put(piece, place_z, core):
        for dh in range(NH):
            spot = ((h + dh) % NH * NZ + (place_z + 2 * NZ) % NZ) * NC + core
            all_ref[pl.ds(pl.multiple_of(spot * ROWS, ROWS), ROWS), :] = piece[dh]

    put(own_pair, z, c)
    put(other_pair, z, 1 - c)
    for r in range(1, 4):
        put(mine.at[r - 1], z - step * r, c)
        put(theirs.at[r - 1], z + step * r, 1 - c)
    for r in range(1, 3):
        put(mine.at[r + 2], z - step * r, 1 - c)
        put(theirs.at[r + 2], z + step * r, c)
    put(last.at[0], z - step * 4, c)
    put(theirs_last.at[0], z + step * 4, 1 - c)
    put(last.at[1], z - step * 3, 1 - c)
    put(theirs_last.at[1], z + step * 3, c)
    for index, part in zip(FIRST, parts):
        part_of(OFFSETS[index], all_ref, w_attn_ref, w_mlp_ref, part)


def parts_kernel(all_ref, w_attn_ref, w_mlp_ref, *parts):
    for index, part in zip(SECOND, parts):
        part_of(OFFSETS[index], all_ref, w_attn_ref, w_mlp_ref, part)


def middle_kernel(qkv_ref, pre_ref, a_ref, b_ref, c_ref, d_ref, grad_ref):
    total = (
        a_ref[...].astype(F32)
        + b_ref[...].astype(F32)
        + c_ref[...].astype(F32)
        + d_ref[...].astype(F32)
    )
    upward = total[:, 0:HD].astype(BF)
    query, key, value = (qkv_ref[:, i * HD : (i + 1) * HD] for i in range(3))
    probs = attn_probs_of(query, key)
    rounded = probs.astype(BF)
    grad_value = dot(rounded, upward, 0, 0)
    grad_probs = dot(upward, value, 1, 1)
    centred = grad_probs - jnp.sum(grad_probs * probs, axis=-1, keepdims=True)
    grad_scores = (probs * centred * (HD**-0.5)).astype(BF)
    grad_ref[:, 0:HD] = dot(grad_scores, key, 1, 0).astype(BF)
    grad_ref[:, HD : 2 * HD] = dot(grad_scores, query, 0, 0).astype(BF)
    grad_ref[:, 2 * HD : 3 * HD] = grad_value.astype(BF)
    pre = pre_ref[...].astype(F32)
    inner = jnp.tanh(GELU_C * (pre + GELU_A * pre * pre * pre))
    slope = 0.5 * (1.0 + inner) + 0.5 * pre * (1.0 - inner * inner) * (
        GELU_C * (1.0 + 3.0 * GELU_A * pre * pre)
    )
    grad_ref[:, 3 * HD :] = (total[:, HD:] * slope).astype(BF)


def sort_rows(take, offsets, mine_ref, other_ref, rows_ref, sem):
    h, z, c = mp_place()
    step = 1 - 2 * c
    w_qkv_ref, w_mlp_ref = take(0), take(1)
    moves = []
    for k, offset in enumerate(offsets):
        grad = take(k + 2)
        image = image_of(offset)
        rows = dot(grad[:, 0 : 3 * HD], w_qkv_ref[...], 1, 1) + dot(
            grad[:, 3 * HD :], w_mlp_ref[...], 1, 1
        )
        rows_ref[k] = rows.astype(BF)
        dh = (image // 4 + h) % NH
        for half in range(2):
            ahead = ((image % 4 * 2 + half - z) * step + NZ) % NZ
            same = jnp.where(ahead <= 4, ahead, 20 - ahead)
            cross = jnp.where(ahead == 0, 8, jnp.where(ahead <= 3, 4 + ahead, 16 - ahead))
            for core in range(2):
                spot = jnp.where(c == core, same, cross)
                index = half * 2 + core
                source = rows_ref.at[k, pl.ds(index * ROWS, ROWS)]
                moves.append((spot, dh, source, sem.at[k, index]))
                move(moves[-1], mine_ref, other_ref, True)
    return moves


def move(one, mine_ref, other_ref, start):
    spot, dh, source, sem = one

    @pl.when(spot < 8)
    def _():
        copy = pltpu.make_async_copy(source, mine_ref.at[spot, dh], sem)
        copy.start() if start else copy.wait()

    @pl.when(spot >= 8)
    def _():
        copy = pltpu.make_async_copy(source, other_ref.at[spot - 8, dh], sem)
        copy.start() if start else copy.wait()


def early_kernel(take, outs, own):
    mine_ref, other_ref, acc_ref = outs
    moves = sort_rows(take, OFFSETS[:4], mine_ref, other_ref, *own)
    in_part(take, OFFSETS[:4], None, acc_ref)
    for one in moves:
        move(one, mine_ref, other_ref, False)


def late_kernel(take, outs, own):
    mine_ref, other_ref, qkv_ref, mlp_ref, gain_ref = outs
    acc_ref = own[2]
    moves = sort_rows(take, OFFSETS[4:], mine_ref, other_ref, *own[:2])
    in_part(take, OFFSETS[4:], take(7), acc_ref)
    qkv = acc_ref[:, 0 : 3 * HD]
    mlp = acc_ref[:, 3 * HD :]
    qkv_ref[...] = qkv.astype(BF)
    mlp_ref[...] = mlp.astype(BF)
    total = 0.0
    for product in (qkv * take(0)[...].astype(F32), mlp * take(1)[...].astype(F32)):
        total = total + lax.dot_general(
            jnp.ones((8, product.shape[1]), F32),
            product,
            (((1,), (1,)), ((), ())),
            precision=lax.Precision.HIGHEST,
            preferred_element_type=F32,
        )
    gain_ref[...] = total
    for one in moves:
        move(one, mine_ref, other_ref, False)


def out_weights_kernel(take, outs, own):
    (attn_ref, mlp_ref), (acc_ref,) = outs, own
    all_ref = take(0)
    for k, offset in enumerate(OFFSETS):
        start = pl.multiple_of(image_of(offset) * PATCH, PATCH)
        term = dot(take(k + 1)[...], all_ref[pl.ds(start, PATCH), :], 0, 0)
        if k == 0:
            acc_ref[...] = term
        else:
            acc_ref[...] += term
    attn_ref[...] = acc_ref[0:HD].astype(BF)
    mlp_ref[...] = acc_ref[HD:].astype(BF)


def in_part(take, offsets, first, acc_ref):
    all_ref = take(6)
    for k, offset in enumerate(offsets):
        start = pl.multiple_of(image_of(offset) * PATCH, PATCH)
        term = dot(all_ref[pl.ds(start, PATCH), :], take(k + 2)[...], 0, 0)
        before = first if k == 0 else acc_ref
        acc_ref[...] = term if before is None else before[...] + term


def add(*terms):
    total = terms[0].astype(F32)
    for term in terms[1:]:
        total = total + term.astype(F32)
    return total.astype(BF)


def gather_dp_first(own):
    return dp_send(own, Y_UP), dp_send(own, Y_DOWN), dp_send(own, X_SWAP)


def gather_dp_second(below, above, beside):
    return dp_send(beside, Y_DOWN), dp_send(beside, Y_UP)


def gather_dp_third(own, below, above, beside, beside_above, beside_below):
    far = dp_send(below, Y_UP)
    beside_far = dp_send(beside_above, Y_DOWN)
    return [own, above, below, beside, far, beside_above, beside_below, beside_far]


def scatter_dp(parts):
    own, above, below, beside, far, beside_above, beside_below, beside_far = parts
    down = dp_send(far, Y_DOWN)
    up = dp_send(beside_far, Y_UP)
    down_beside = dp_send(beside_below, Y_DOWN)
    up_beside = dp_send(add(beside_above, up), Y_UP)
    down_last = dp_send(add(below, down), Y_DOWN)
    up_last = dp_send(above, Y_UP)
    across = dp_send(add(beside, down_beside, up_beside), X_SWAP)
    return own, down_last, up_last, across


def join_stats(mean, square, count, theirs):
    means = [mean] + [one[0] for one in theirs]
    squares = [square] + [one[1] for one in theirs]
    joined = sum(means) / len(means)
    spread = sum(jnp.square(one - joined) for one in means)
    return joined, sum(squares) + count * spread


def gather_mp(own, act, widened):
    width = widened.shape[1]
    mean = jnp.mean(widened, axis=1)
    square = jnp.sum(jnp.square(widened - mean[:, None]), axis=1)
    theirs = dp_send(jnp.stack([mean, square]), X_SWAP)
    own_pair = jnp.stack([own, mp_send(own, H_SWAP)])
    own_pair, theirs, act = lax.optimization_barrier((own_pair, theirs, act))
    mean, square = join_stats(mean, square, width, [theirs])
    stats = jnp.stack([mean, square])
    theirs = [dp_send(stats, perm) for perm in (Y_UP, Y_DOWN, Y_TWO)]
    other_pair = mp_send(own_pair, C_SWAP)
    mine_a = [mp_send(own_pair, Z_RING)]
    mine_a, other_pair, theirs, act = lax.optimization_barrier((mine_a, other_pair, theirs, act))
    stats = join_stats(mean, square, 2 * width, theirs)
    first = gather_dp_first(act)
    mine_b = [mp_send(other_pair, Z_RING)]
    mine_a.append(mp_send(mine_a[-1], Z_RING))
    mine_a.append(mp_send(mine_a[-1], Z_RING))
    mine_b.append(mp_send(mine_b[-1], Z_RING))
    mine_a, mine_b, first = lax.optimization_barrier((mine_a, mine_b, first))
    second = gather_dp_second(*first)
    mine = jnp.stack(mine_a + mine_b)
    last = jnp.stack([mp_send(mine_a[-1], Z_RING), mp_send(mine_b[-1], Z_RING)])
    theirs = mp_send(mine, C_SWAP)
    last, theirs, second = lax.optimization_barrier((last, theirs, second))
    theirs_last = mp_send(last, C_SWAP)
    pieces = [own_pair, other_pair, mine, last, theirs, theirs_last]
    return pieces, gather_dp_third(act, *first, *second), stats


def pack(value):
    high = lax.reduce_precision(value, 8, 7)
    middle = lax.reduce_precision(value - high, 8, 7)
    rows = jnp.stack([high, middle, value - high - middle]).astype(BF)
    return jnp.pad(rows, ((0, 13), (0, 0)))


def unpack(rows):
    rows = rows.astype(F32)
    return rows[0] + rows[1] + rows[2]


def with_rows(block, *rows):
    return jnp.concatenate([block.reshape(-1, block.shape[-1]), *rows])


def scatter_mp(mine, other, gain, acts, finish):
    height = 2 * ROWS
    received = mp_send(other, C_SWAP)
    gain = gain + mp_send(gain, C_SWAP)
    received, gain = lax.optimization_barrier((received, gain))
    held = add(mine, received)
    got = mp_send(with_rows(held[4], pack(gain)), Z_RING)
    ring_b = mp_send(held[7], Z_RING)
    passed = []
    for step in range(3):
        rows = got[height:]
        passed.append(rows)
        block = add(held[3 - step].reshape(height, -1), got[:height])
        got = mp_send(with_rows(block, rows), Z_RING)
        if step < 2:
            ring_b = mp_send(add(held[6 - step], ring_b), Z_RING)
            if step == 1:
                got, acts = lax.optimization_barrier((got, acts))
        else:
            ring_b = mp_send(with_rows(ring_b, *passed), C_SWAP)
    ring_a = got[:height].reshape(NH, ROWS, -1)
    opposite = ring_b[height:]
    ring_b = ring_b[:height].reshape(NH, ROWS, -1)
    _, z, c = mp_place()
    step = 1 - 2 * c
    sums = [(z, gain), (z + 4, unpack(got[height:]))]
    for r in range(3):
        sums.append((z - step * (r + 1), unpack(passed[r])))
        sums.append((z + step * (r + 1), unpack(opposite[16 * r : 16 * r + 16])))
    spots = jnp.arange(NZ)[:, None]
    ordered = sum(jnp.where(spots == (at + NZ) % NZ, one[None, :], 0.0) for at, one in sums)
    gain = ordered[0]
    for index in range(1, NZ):
        gain = gain + ordered[index]
    across = mp_send(
        with_rows(add(held[0, 1], ring_a[1], ring_b[1]), pack(gain)), H_SWAP
    )
    across, tied = lax.optimization_barrier((across, finish(acts)))
    total = across[:ROWS].astype(F32)
    for term in (held[0, 0], ring_a[0], ring_b[0]):
        total = total + term.astype(F32)
    gain = unpack(pack(gain)) + unpack(across[ROWS:])
    return total, tied, gain


def sum_dp(values):
    values = values + dp_send(values, X_SWAP)
    others = [dp_send(values, perm) for perm in (Y_UP, Y_DOWN, Y_TWO)]
    return values + others[0] + others[1] + others[2]


def per_device(
    block_input, ln_gain, qkv_act, mlp_pre, out_grad, w_qkv, w_mlp, w_out_attn, w_out_mlp
):
    shape = jax.ShapeDtypeStruct
    widened = block_input.astype(F32)
    act = call(
        forward_kernel, shape((PATCH, 896), BF), 2, 10, flops=10**8, nbytes=2 * 10**6
    )(qkv_act, mlp_pre)
    pieces, all_acts, (mean, square) = gather_mp(out_grad, act, widened)
    inverse = lax.rsqrt(square / D + eps)
    normed = (widened - mean[:, None]) * inverse[:, None]
    scaled = (normed * ln_gain[None, :]).astype(BF)
    all_scaled = lax.all_gather(scaled, "mp", axis=0, tiled=True)
    part_shape = [shape((PATCH, 896), BF)] * 4
    all_grad, *first = call(
        spread_kernel,
        [shape((2048, 768), BF)] + part_shape,
        8,
        16,
        flops=2048 * 768 * 896,
        nbytes=10 * 10**6,
    )(*pieces, w_out_attn, w_out_mlp)
    second = call(parts_kernel, part_shape, 3, 14, flops=2048 * 768 * 896, nbytes=6 * 10**6)(
        all_grad, w_out_attn, w_out_mlp
    )
    parts = [None] * 8
    for index, part in zip(FIRST + SECOND, first + list(second)):
        parts[index] = part
    sums = scatter_dp(parts)
    grad = call(
        middle_kernel, shape((PATCH, 1152), BF), 6, 14, flops=2 * 10**8, nbytes=3 * 10**6
    )(qkv_act, mlp_pre, *sums)
    near = gather_dp_first(grad)
    near, all_scaled = lax.optimization_barrier((near, all_scaled))
    grads = gather_dp_third(grad, *near, *gather_dp_second(*near))
    early, late = grads[:4], grads[4:]
    slots = [shape((8, NH, ROWS, 768), BF)] * 2
    sort_scratch = [pltpu.VMEM((4, PATCH, 768), BF), pltpu.SemaphoreType.DMA((4, 4))]
    mine, other, acc_half = staged_call(
        early_kernel,
        [*slots, shape((768, 1152), F32)],
        [w_qkv, w_mlp, *early, all_scaled],
        24,
        2 * 2048 * 768 * 1152,
        12 * 10**6,
        scratch=sort_scratch,
        any_out=2,
        staged=False,
    )
    late, mine = lax.optimization_barrier((late, mine))
    mine, other, acc_qkv, acc_pre, gain_part = staged_call(
        late_kernel,
        [*slots, shape((768, 384), BF), shape((768, 768), BF), shape((8, 768), F32)],
        [mine, other, w_qkv, w_mlp, *late, all_scaled, acc_half],
        30,
        2 * 2048 * 768 * 1152,
        16 * 10**6,
        scratch=[*sort_scratch, pltpu.VMEM((768, 1152), F32)],
        held=2,
        any_out=2,
        staged=False,
    )

    def finish(acts):
        return staged_call(
            out_weights_kernel,
            [shape((HD, 768), BF), shape((768, 768), BF)],
            [all_grad, *acts],
            60,
            2 * 2048 * 768 * 896,
            8 * 10**6,
            scratch=[pltpu.VMEM((896, 768), F32)],
        )

    grad_normed, (acc_attn, acc_mlp), gain_grad = scatter_mp(
        mine, other, gain_part[0] / ln_gain, all_acts, finish
    )
    weighted = grad_normed * ln_gain[None, :]
    sums = jnp.stack([jnp.sum(weighted, axis=1), jnp.sum(weighted * normed, axis=1)])
    sums = sum_dp(sums) / D
    input_grad = out_grad.astype(F32) + inverse[:, None] * (
        weighted - sums[0][:, None] - normed * sums[1][:, None]
    )
    return (input_grad.astype(BF), acc_qkv, acc_pre, acc_attn, acc_mlp, gain_grad)


def solution(mesh):
    return jax.shard_map(
        per_device,
        mesh=mesh,
        in_specs=(
            P("mp", "dp"),
            P("dp"),
            P("dp", "mp"),
            P("dp", "mp"),
            P("mp", "dp"),
            P("dp", "mp"),
            P("dp", "mp"),
            P("mp", "dp"),
            P("mp", "dp"),
        ),
        out_specs=(
            P("mp", "dp"),
            P("dp", "mp"),
            P("dp", "mp"),
            P("mp", "dp"),
            P("mp", "dp"),
            P("dp"),
        ),
        check_vma=False,
    )
```

```python
import jax
import jax.numpy as jnp
from jax import lax
from jax.experimental import pallas as pl
from jax.experimental.pallas import tpu as pltpu
from jax.sharding import PartitionSpec as P

D = 6144
HD = 128
PATCH = 256
eps = 1e-06
BF = jnp.bfloat16
F32 = jnp.float32

NY, NX, NH, NZ, NC = 4, 2, 2, 8, 2
ROWS = 64


def dp_perm(move):
    pairs = []
    for y in range(NY):
        for x in range(NX):
            to_y, to_x = move(y, x)
            pairs.append((y * NX + x, (to_y % NY) * NX + to_x))
    return pairs


def mp_perm(move):
    pairs = []
    for h in range(NH):
        for z in range(NZ):
            for c in range(NC):
                to_h, to_z, to_c = move(h, z, c)
                pairs.append(((h * NZ + z) * NC + c, (to_h * NZ + to_z % NZ) * NC + to_c))
    return pairs


X_SWAP = dp_perm(lambda y, x: (y, 1 - x))
Y_UP = dp_perm(lambda y, x: (y + 1, x))
Y_DOWN = dp_perm(lambda y, x: (y - 1, x))
Y_TWO = dp_perm(lambda y, x: (y ^ 2, x))
H_SWAP = mp_perm(lambda h, z, c: (1 - h, z, c))
C_SWAP = mp_perm(lambda h, z, c: (h, z, 1 - c))
Z_RING = mp_perm(lambda h, z, c: (h, z + 1 - 2 * c, c))

OFFSETS = [(0, 0), (1, 0), (3, 0), (0, 1), (2, 0), (1, 1), (3, 1), (2, 1)]


def dp_send(array, perm):
    return lax.ppermute(array, "dp", perm)


def mp_send(array, perm):
    return lax.ppermute(array, "mp", perm)


def dp_place():
    index = lax.axis_index("dp")
    return index // NX, index % NX


def mp_place():
    index = lax.axis_index("mp")
    return index // (NZ * NC), (index // NC) % NZ, index % NC


def image_of(offset):
    y, x = dp_place()
    dy, dx = offset
    return ((y + dy) % NY) * NX + (x + dx) % NX


def dot(a, b, ca, cb):
    return lax.dot_general(a, b, (((ca,), (cb,)), ((), ())), preferred_element_type=F32)


def call(kernel, out_shape, n_in, limit, flops=0, nbytes=0):
    return pl.pallas_call(
        kernel,
        out_shape=out_shape,
        in_specs=[pl.BlockSpec(memory_space=pltpu.VMEM)] * n_in,
        out_specs=jax.tree.map(lambda _: pl.BlockSpec(memory_space=pltpu.VMEM), out_shape),
        compiler_params=pltpu.CompilerParams(vmem_limit_bytes=limit * 1024 * 1024),
        cost_estimate=pl.CostEstimate(flops=flops, bytes_accessed=nbytes, transcendentals=0),
    )


def staged_call(
    kernel, out_shape, args, limit, flops, nbytes, scratch=(), held=0, any_out=0, staged=True
):
    moved = args[held:] if staged else []

    def body(*refs):
        sources, rest = refs[held : len(args)], refs[len(args) :]
        outs, rest = rest[: len(out_shape)], rest[len(out_shape) :]
        own, buffers = rest[: len(scratch)], rest[len(scratch) : len(scratch) + len(moved)]
        if not staged:
            kernel(lambda i: sources[i], outs, own)
            return
        sem = rest[-1]
        copies = [
            pltpu.make_async_copy(source, buffer, sem.at[i])
            for i, (source, buffer) in enumerate(zip(sources, buffers))
        ]
        for copy in copies:
            copy.start()

        def take(i):
            copies[i].wait()
            return buffers[i]

        kernel(take, outs, own)

    return pl.pallas_call(
        body,
        out_shape=out_shape,
        in_specs=[pl.BlockSpec(memory_space=pl.ANY)] * held
        + [pl.BlockSpec(memory_space=pl.ANY if staged else pltpu.VMEM)] * (len(args) - held),
        out_specs=[
            pl.BlockSpec(memory_space=pl.ANY if i < any_out else pltpu.VMEM)
            for i in range(len(out_shape))
        ],
        scratch_shapes=list(scratch)
        + [pltpu.VMEM(one.shape, one.dtype) for one in moved]
        + [pltpu.SemaphoreType.DMA((len(moved),))] * staged,
        input_output_aliases={i: i for i in range(held)},
        compiler_params=pltpu.CompilerParams(vmem_limit_bytes=limit * 1024 * 1024),
        cost_estimate=pl.CostEstimate(flops=flops, bytes_accessed=nbytes, transcendentals=0),
    )(*args)


GELU_C = 0.7978845608028654
GELU_A = 0.044715


def attn_probs_of(query, key):
    scores = dot(query, key, 1, 1) * (HD**-0.5)
    scores = scores - jnp.max(scores, axis=-1, keepdims=True)
    powers = jnp.exp(scores)
    return powers / jnp.sum(powers, axis=-1, keepdims=True)


def forward_kernel(qkv_ref, pre_ref, act_ref):
    probs = attn_probs_of(qkv_ref[:, 0:HD], qkv_ref[:, HD : 2 * HD])
    attended = dot(probs.astype(BF), qkv_ref[:, 2 * HD : 3 * HD], 1, 0)
    act_ref[:, 0:HD] = attended.astype(BF)
    pre = pre_ref[...].astype(F32)
    inner = jnp.tanh(GELU_C * (pre + GELU_A * pre * pre * pre))
    act_ref[:, HD:] = (0.5 * pre * (1.0 + inner)).astype(BF)


def part_of(offset, all_ref, w_attn_ref, w_mlp_ref, part):
    start = pl.multiple_of(image_of(offset) * PATCH, PATCH)
    rows = all_ref[pl.ds(start, PATCH), :]
    part[:, 0:HD] = dot(rows, w_attn_ref[...], 1, 1).astype(BF)
    part[:, HD:] = dot(rows, w_mlp_ref[...], 1, 1).astype(BF)


FIRST = [4, 7, 6, 1]
SECOND = [5, 2, 3, 0]


def spread_kernel(*refs):
    pieces, (w_attn_ref, w_mlp_ref, all_ref), parts = refs[:6], refs[6:9], refs[9:]
    own_pair, other_pair, mine, last, theirs, theirs_last = pieces
    h, z, c = mp_place()
    step = 1 - 2 * c

    def put(piece, place_z, core):
        for dh in range(NH):
            spot = ((h + dh) % NH * NZ + (place_z + 2 * NZ) % NZ) * NC + core
            all_ref[pl.ds(pl.multiple_of(spot * ROWS, ROWS), ROWS), :] = piece[dh]

    put(own_pair, z, c)
    put(other_pair, z, 1 - c)
    for r in range(1, 4):
        put(mine.at[r - 1], z - step * r, c)
        put(theirs.at[r - 1], z + step * r, 1 - c)
    for r in range(1, 3):
        put(mine.at[r + 2], z - step * r, 1 - c)
        put(theirs.at[r + 2], z + step * r, c)
    put(last.at[0], z - step * 4, c)
    put(theirs_last.at[0], z + step * 4, 1 - c)
    put(last.at[1], z - step * 3, 1 - c)
    put(theirs_last.at[1], z + step * 3, c)
    for index, part in zip(FIRST, parts):
        part_of(OFFSETS[index], all_ref, w_attn_ref, w_mlp_ref, part)


def parts_kernel(all_ref, w_attn_ref, w_mlp_ref, *parts):
    for index, part in zip(SECOND, parts):
        part_of(OFFSETS[index], all_ref, w_attn_ref, w_mlp_ref, part)


def middle_kernel(qkv_ref, pre_ref, a_ref, b_ref, c_ref, d_ref, grad_ref):
    total = (
        a_ref[...].astype(F32)
        + b_ref[...].astype(F32)
        + c_ref[...].astype(F32)
        + d_ref[...].astype(F32)
    )
    upward = total[:, 0:HD].astype(BF)
    query, key, value = (qkv_ref[:, i * HD : (i + 1) * HD] for i in range(3))
    probs = attn_probs_of(query, key)
    rounded = probs.astype(BF)
    grad_value = dot(rounded, upward, 0, 0)
    grad_probs = dot(upward, value, 1, 1)
    centred = grad_probs - jnp.sum(grad_probs * probs, axis=-1, keepdims=True)
    grad_scores = (probs * centred * (HD**-0.5)).astype(BF)
    grad_ref[:, 0:HD] = dot(grad_scores, key, 1, 0).astype(BF)
    grad_ref[:, HD : 2 * HD] = dot(grad_scores, query, 0, 0).astype(BF)
    grad_ref[:, 2 * HD : 3 * HD] = grad_value.astype(BF)
    pre = pre_ref[...].astype(F32)
    inner = jnp.tanh(GELU_C * (pre + GELU_A * pre * pre * pre))
    slope = 0.5 * (1.0 + inner) + 0.5 * pre * (1.0 - inner * inner) * (
        GELU_C * (1.0 + 3.0 * GELU_A * pre * pre)
    )
    grad_ref[:, 3 * HD :] = (total[:, HD:] * slope).astype(BF)


def sort_rows(take, offsets, mine_ref, other_ref, rows_ref, sem):
    h, z, c = mp_place()
    step = 1 - 2 * c
    w_qkv_ref, w_mlp_ref = take(0), take(1)
    moves = []
    for k, offset in enumerate(offsets):
        grad = take(k + 2)
        image = image_of(offset)
        rows = dot(grad[:, 0 : 3 * HD], w_qkv_ref[...], 1, 1) + dot(
            grad[:, 3 * HD :], w_mlp_ref[...], 1, 1
        )
        rows_ref[k] = rows.astype(BF)
        dh = (image // 4 + h) % NH
        for half in range(2):
            ahead = ((image % 4 * 2 + half - z) * step + NZ) % NZ
            same = jnp.where(ahead <= 4, ahead, 20 - ahead)
            cross = jnp.where(ahead == 0, 8, jnp.where(ahead <= 3, 4 + ahead, 16 - ahead))
            for core in range(2):
                spot = jnp.where(c == core, same, cross)
                index = half * 2 + core
                source = rows_ref.at[k, pl.ds(index * ROWS, ROWS)]
                moves.append((spot, dh, source, sem.at[k, index]))
                move(moves[-1], mine_ref, other_ref, True)
    return moves


def move(one, mine_ref, other_ref, start):
    spot, dh, source, sem = one

    @pl.when(spot < 8)
    def _():
        copy = pltpu.make_async_copy(source, mine_ref.at[spot, dh], sem)
        copy.start() if start else copy.wait()

    @pl.when(spot >= 8)
    def _():
        copy = pltpu.make_async_copy(source, other_ref.at[spot - 8, dh], sem)
        copy.start() if start else copy.wait()


def early_kernel(take, outs, own):
    mine_ref, other_ref, acc_ref = outs
    moves = sort_rows(take, OFFSETS[:4], mine_ref, other_ref, *own)
    in_part(take, OFFSETS[:4], None, acc_ref)
    for one in moves:
        move(one, mine_ref, other_ref, False)


def late_kernel(take, outs, own):
    mine_ref, other_ref, qkv_ref, mlp_ref, gain_ref = outs
    acc_ref = own[2]
    moves = sort_rows(take, OFFSETS[4:], mine_ref, other_ref, *own[:2])
    in_part(take, OFFSETS[4:], take(7), acc_ref)
    qkv = acc_ref[:, 0 : 3 * HD]
    mlp = acc_ref[:, 3 * HD :]
    qkv_ref[...] = qkv.astype(BF)
    mlp_ref[...] = mlp.astype(BF)
    total = 0.0
    for product in (qkv * take(0)[...].astype(F32), mlp * take(1)[...].astype(F32)):
        for at in range(0, product.shape[1], 128):
            total = total + product[:, at : at + 128]
    total = jnp.broadcast_to(jnp.sum(total.T, axis=0, keepdims=True), gain_ref.shape)
    gain_ref[...] = total
    for one in moves:
        move(one, mine_ref, other_ref, False)


def out_weights_kernel(*refs):
    acts, (all_ref, attn_ref, mlp_ref, acc_ref, act_buffer, row_buffer, sem) = refs[:8], refs[8:]
    copies = []
    for k, offset in enumerate(OFFSETS):
        start = pl.multiple_of(image_of(offset) * PATCH, PATCH)
        copies.append(pltpu.make_async_copy(acts[k], act_buffer.at[k], sem.at[0, k]))
        copies.append(
            pltpu.make_async_copy(all_ref.at[pl.ds(start, PATCH)], row_buffer.at[k], sem.at[1, k])
        )
    for copy in copies:
        copy.start()
    for k in range(8):
        copies[2 * k].wait()
        copies[2 * k + 1].wait()
        term = dot(act_buffer[k], row_buffer[k], 0, 0)
        if k == 0:
            acc_ref[...] = term
        else:
            acc_ref[...] += term
    attn_ref[...] = acc_ref[0:HD].astype(BF)
    mlp_ref[...] = acc_ref[HD:].astype(BF)


def in_part(take, offsets, first, acc_ref):
    all_ref = take(6)
    for k, offset in enumerate(offsets):
        start = pl.multiple_of(image_of(offset) * PATCH, PATCH)
        term = dot(all_ref[pl.ds(start, PATCH), :], take(k + 2)[...], 0, 0)
        before = first if k == 0 else acc_ref
        acc_ref[...] = term if before is None else before[...] + term


def add(*terms):
    total = terms[0].astype(F32)
    for term in terms[1:]:
        total = total + term.astype(F32)
    return total.astype(BF)


def gather_dp_first(own):
    return dp_send(own, Y_UP), dp_send(own, Y_DOWN), dp_send(own, X_SWAP)


def gather_dp_second(below, above, beside):
    return dp_send(beside, Y_DOWN), dp_send(beside, Y_UP)


def gather_dp_third(own, below, above, beside, beside_above, beside_below):
    far = dp_send(below, Y_UP)
    beside_far = dp_send(beside_above, Y_DOWN)
    return [own, above, below, beside, far, beside_above, beside_below, beside_far]


def scatter_dp(parts):
    own, above, below, beside, far, beside_above, beside_below, beside_far = parts
    down = dp_send(far, Y_DOWN)
    up = dp_send(beside_far, Y_UP)
    down_beside = dp_send(beside_below, Y_DOWN)
    up_beside = dp_send(add(beside_above, up), Y_UP)
    down_last = dp_send(add(below, down), Y_DOWN)
    up_last = dp_send(above, Y_UP)
    across = dp_send(add(beside, down_beside, up_beside), X_SWAP)
    return own, down_last, up_last, across


def join_stats(mean, square, count, theirs):
    means = [mean] + [one[0] for one in theirs]
    squares = [square] + [one[1] for one in theirs]
    joined = sum(means) / len(means)
    spread = sum(jnp.square(one - joined) for one in means)
    return joined, sum(squares) + count * spread


def gather_mp(own, act, widened):
    width = widened.shape[1]
    mean = jnp.mean(widened, axis=1)
    square = jnp.sum(jnp.square(widened - mean[:, None]), axis=1)
    theirs = dp_send(jnp.stack([mean, square]), X_SWAP)
    own_pair = jnp.stack([own, mp_send(own, H_SWAP)])
    own_pair, theirs, act = lax.optimization_barrier((own_pair, theirs, act))
    mean, square = join_stats(mean, square, width, [theirs])
    stats = jnp.stack([mean, square])
    theirs = [dp_send(stats, perm) for perm in (Y_UP, Y_DOWN, Y_TWO)]
    other_pair = mp_send(own_pair, C_SWAP)
    mine_a = [mp_send(own_pair, Z_RING)]
    mine_a, other_pair, theirs, act = lax.optimization_barrier((mine_a, other_pair, theirs, act))
    stats = join_stats(mean, square, 2 * width, theirs)
    first = gather_dp_first(act)
    mine_b = [mp_send(other_pair, Z_RING)]
    mine_a.append(mp_send(mine_a[-1], Z_RING))
    mine_a.append(mp_send(mine_a[-1], Z_RING))
    mine_b.append(mp_send(mine_b[-1], Z_RING))
    mine_a, mine_b, first = lax.optimization_barrier((mine_a, mine_b, first))
    second = gather_dp_second(*first)
    mine = jnp.stack(mine_a + mine_b)
    last = jnp.stack([mp_send(mine_a[-1], Z_RING), mp_send(mine_b[-1], Z_RING)])
    theirs = mp_send(mine, C_SWAP)
    last, theirs, second = lax.optimization_barrier((last, theirs, second))
    theirs_last = mp_send(last, C_SWAP)
    pieces = [own_pair, other_pair, mine, last, theirs, theirs_last]
    return pieces, gather_dp_third(act, *first, *second), stats


def pack(value):
    high = lax.reduce_precision(value, 8, 7)
    middle = lax.reduce_precision(value - high, 8, 7)
    rows = jnp.stack([high, middle, value - high - middle]).astype(BF)
    return jnp.pad(rows, ((0, 13), (0, 0)))


def unpack(rows):
    rows = rows.astype(F32)
    return rows[0] + rows[1] + rows[2]


def with_rows(block, *rows):
    return jnp.concatenate([block.reshape(-1, block.shape[-1]), *rows])


def scatter_mp(mine, other, gain, acts, finish):
    height = 2 * ROWS
    received = mp_send(other, C_SWAP)
    gain = gain + mp_send(gain, C_SWAP)
    received, gain = lax.optimization_barrier((received, gain))
    held = add(mine, received)
    got = mp_send(with_rows(held[4], pack(gain)), Z_RING)
    ring_b = mp_send(held[7], Z_RING)
    passed = []
    for step in range(3):
        rows = got[height:]
        passed.append(rows)
        block = add(held[3 - step].reshape(height, -1), got[:height])
        got = mp_send(with_rows(block, rows), Z_RING)
        if step < 2:
            ring_b = mp_send(add(held[6 - step], ring_b), Z_RING)
            if step == 1:
                got, acts = lax.optimization_barrier((got, acts))
        else:
            ring_b = mp_send(with_rows(ring_b, *passed), C_SWAP)
    ring_a = got[:height].reshape(NH, ROWS, -1)
    opposite = ring_b[height:]
    ring_b = ring_b[:height].reshape(NH, ROWS, -1)
    _, z, c = mp_place()
    step = 1 - 2 * c
    sums = [(z, gain), (z + 4, unpack(got[height:]))]
    for r in range(3):
        sums.append((z - step * (r + 1), unpack(passed[r])))
        sums.append((z + step * (r + 1), unpack(opposite[16 * r : 16 * r + 16])))
    spots = jnp.arange(NZ)[:, None]
    ordered = sum(jnp.where(spots == (at + NZ) % NZ, one[None, :], 0.0) for at, one in sums)
    gain = ordered[0]
    for index in range(1, NZ):
        gain = gain + ordered[index]
    across = mp_send(
        with_rows(add(held[0, 1], ring_a[1], ring_b[1]), pack(gain)), H_SWAP
    )
    across, tied = lax.optimization_barrier((across, finish(acts)))
    total = across[:ROWS].astype(F32)
    for term in (held[0, 0], ring_a[0], ring_b[0]):
        total = total + term.astype(F32)
    gain = unpack(pack(gain)) + unpack(across[ROWS:])
    return total, tied, gain


def sum_dp(values):
    values = values + dp_send(values, X_SWAP)
    others = [dp_send(values, perm) for perm in (Y_UP, Y_DOWN, Y_TWO)]
    return values + others[0] + others[1] + others[2]


def per_device(
    block_input, ln_gain, qkv_act, mlp_pre, out_grad, w_qkv, w_mlp, w_out_attn, w_out_mlp
):
    shape = jax.ShapeDtypeStruct
    widened = block_input.astype(F32)
    act = call(
        forward_kernel, shape((PATCH, 896), BF), 2, 10, flops=10**8, nbytes=2 * 10**6
    )(qkv_act, mlp_pre)
    pieces, all_acts, (mean, square) = gather_mp(out_grad, act, widened)
    inverse = lax.rsqrt(square / D + eps)
    normed = (widened - mean[:, None]) * inverse[:, None]
    scaled = (normed * ln_gain[None, :]).astype(BF)
    all_scaled = lax.all_gather(scaled, "mp", axis=0, tiled=True)
    part_shape = [shape((PATCH, 896), BF)] * 4
    all_grad, *first = call(
        spread_kernel,
        [shape((2048, 768), BF)] + part_shape,
        8,
        16,
        flops=2048 * 768 * 896,
        nbytes=10 * 10**6,
    )(*pieces, w_out_attn, w_out_mlp)
    second = call(parts_kernel, part_shape, 3, 14, flops=2048 * 768 * 896, nbytes=6 * 10**6)(
        all_grad, w_out_attn, w_out_mlp
    )
    parts = [None] * 8
    for index, part in zip(FIRST + SECOND, first + list(second)):
        parts[index] = part
    sums = scatter_dp(parts)
    grad = call(
        middle_kernel, shape((PATCH, 1152), BF), 6, 14, flops=2 * 10**8, nbytes=3 * 10**6
    )(qkv_act, mlp_pre, *sums)
    near = gather_dp_first(grad)
    near, all_scaled = lax.optimization_barrier((near, all_scaled))
    grads = gather_dp_third(grad, *near, *gather_dp_second(*near))
    early, late = grads[:4], grads[4:]
    slots = [shape((8, NH, ROWS, 768), BF)] * 2
    sort_scratch = [pltpu.VMEM((4, PATCH, 768), BF), pltpu.SemaphoreType.DMA((4, 4))]
    mine, other, acc_half = staged_call(
        early_kernel,
        [*slots, shape((768, 1152), F32)],
        [w_qkv, w_mlp, *early, all_scaled],
        24,
        2 * 2048 * 768 * 1152,
        12 * 10**6,
        scratch=sort_scratch,
        any_out=2,
        staged=False,
    )
    late, mine = lax.optimization_barrier((late, mine))
    mine, other, acc_qkv, acc_pre, gain_part = staged_call(
        late_kernel,
        [*slots, shape((768, 384), BF), shape((768, 768), BF), shape((8, 768), F32)],
        [mine, other, w_qkv, w_mlp, *late, all_scaled, acc_half],
        30,
        2 * 2048 * 768 * 1152,
        16 * 10**6,
        scratch=[*sort_scratch, pltpu.VMEM((768, 1152), F32)],
        held=2,
        any_out=2,
        staged=False,
    )

    def finish(acts):
        return pl.pallas_call(
            out_weights_kernel,
            out_shape=[shape((HD, 768), BF), shape((768, 768), BF)],
            in_specs=[pl.BlockSpec(memory_space=pl.ANY)] * 9,
            out_specs=[pl.BlockSpec(memory_space=pltpu.VMEM)] * 2,
            scratch_shapes=[
                pltpu.VMEM((896, 768), F32),
                pltpu.VMEM((8, PATCH, 896), BF),
                pltpu.VMEM((8, PATCH, 768), BF),
                pltpu.SemaphoreType.DMA((2, 8)),
            ],
            compiler_params=pltpu.CompilerParams(vmem_limit_bytes=60 * 1024 * 1024),
            cost_estimate=pl.CostEstimate(
                flops=2 * 2048 * 768 * 896, bytes_accessed=8 * 10**6, transcendentals=0
            ),
        )(*acts, all_grad)

    grad_normed, (acc_attn, acc_mlp), gain_grad = scatter_mp(
        mine, other, gain_part[0] / ln_gain, all_acts, finish
    )
    weighted = grad_normed * ln_gain[None, :]
    sums = jnp.stack([jnp.sum(weighted, axis=1), jnp.sum(weighted * normed, axis=1)])
    sums = sum_dp(sums) / D
    input_grad = out_grad.astype(F32) + inverse[:, None] * (
        weighted - sums[0][:, None] - normed * sums[1][:, None]
    )
    return (input_grad.astype(BF), acc_qkv, acc_pre, acc_attn, acc_mlp, gain_grad)


def solution(mesh):
    return jax.shard_map(
        per_device,
        mesh=mesh,
        in_specs=(
            P("mp", "dp"),
            P("dp"),
            P("dp", "mp"),
            P("dp", "mp"),
            P("mp", "dp"),
            P("dp", "mp"),
            P("dp", "mp"),
            P("mp", "dp"),
            P("mp", "dp"),
        ),
        out_specs=(
            P("mp", "dp"),
            P("dp", "mp"),
            P("dp", "mp"),
            P("mp", "dp"),
            P("mp", "dp"),
            P("dp"),
        ),
        check_vma=False,
    )
```

```python
import jax
import jax.numpy as jnp
from jax import lax
from jax.experimental import pallas as pl
from jax.experimental.pallas import tpu as pltpu
from jax.sharding import PartitionSpec as P

D = 6144
HD = 128
PATCH = 256
eps = 1e-06
BF = jnp.bfloat16
F32 = jnp.float32

NY, NX, NH, NZ, NC = 4, 2, 2, 8, 2
ROWS = 64


def dp_perm(move):
    pairs = []
    for y in range(NY):
        for x in range(NX):
            to_y, to_x = move(y, x)
            pairs.append((y * NX + x, (to_y % NY) * NX + to_x))
    return pairs


def mp_perm(move):
    pairs = []
    for h in range(NH):
        for z in range(NZ):
            for c in range(NC):
                to_h, to_z, to_c = move(h, z, c)
                pairs.append(((h * NZ + z) * NC + c, (to_h * NZ + to_z % NZ) * NC + to_c))
    return pairs


X_SWAP = dp_perm(lambda y, x: (y, 1 - x))
Y_UP = dp_perm(lambda y, x: (y + 1, x))
Y_DOWN = dp_perm(lambda y, x: (y - 1, x))
Y_TWO = dp_perm(lambda y, x: (y ^ 2, x))
H_SWAP = mp_perm(lambda h, z, c: (1 - h, z, c))
C_SWAP = mp_perm(lambda h, z, c: (h, z, 1 - c))
Z_RING = mp_perm(lambda h, z, c: (h, z + 1 - 2 * c, c))

OFFSETS = [(0, 0), (1, 0), (3, 0), (0, 1), (2, 0), (1, 1), (3, 1), (2, 1)]


def dp_send(array, perm):
    return lax.ppermute(array, "dp", perm)


def mp_send(array, perm):
    return lax.ppermute(array, "mp", perm)


def dp_place():
    index = lax.axis_index("dp")
    return index // NX, index % NX


def mp_place():
    index = lax.axis_index("mp")
    return index // (NZ * NC), (index // NC) % NZ, index % NC


def image_of(offset):
    y, x = dp_place()
    dy, dx = offset
    return ((y + dy) % NY) * NX + (x + dx) % NX


def dot(a, b, ca, cb):
    return lax.dot_general(a, b, (((ca,), (cb,)), ((), ())), preferred_element_type=F32)


def call(kernel, out_shape, n_in, limit, flops=0, nbytes=0):
    return pl.pallas_call(
        kernel,
        out_shape=out_shape,
        in_specs=[pl.BlockSpec(memory_space=pltpu.VMEM)] * n_in,
        out_specs=jax.tree.map(lambda _: pl.BlockSpec(memory_space=pltpu.VMEM), out_shape),
        compiler_params=pltpu.CompilerParams(vmem_limit_bytes=limit * 1024 * 1024),
        cost_estimate=pl.CostEstimate(flops=flops, bytes_accessed=nbytes, transcendentals=0),
    )


def staged_call(
    kernel, out_shape, args, limit, flops, nbytes, scratch=(), held=0, any_out=0, staged=True
):
    moved = args[held:] if staged else []

    def body(*refs):
        sources, rest = refs[held : len(args)], refs[len(args) :]
        outs, rest = rest[: len(out_shape)], rest[len(out_shape) :]
        own, buffers = rest[: len(scratch)], rest[len(scratch) : len(scratch) + len(moved)]
        if not staged:
            kernel(lambda i: sources[i], outs, own)
            return
        sem = rest[-1]
        copies = [
            pltpu.make_async_copy(source, buffer, sem.at[i])
            for i, (source, buffer) in enumerate(zip(sources, buffers))
        ]
        for copy in copies:
            copy.start()

        def take(i):
            copies[i].wait()
            return buffers[i]

        kernel(take, outs, own)

    return pl.pallas_call(
        body,
        out_shape=out_shape,
        in_specs=[pl.BlockSpec(memory_space=pl.ANY)] * held
        + [pl.BlockSpec(memory_space=pl.ANY if staged else pltpu.VMEM)] * (len(args) - held),
        out_specs=[
            pl.BlockSpec(memory_space=pl.ANY if i < any_out else pltpu.VMEM)
            for i in range(len(out_shape))
        ],
        scratch_shapes=list(scratch)
        + [pltpu.VMEM(one.shape, one.dtype) for one in moved]
        + [pltpu.SemaphoreType.DMA((len(moved),))] * staged,
        input_output_aliases={i: i for i in range(held)},
        compiler_params=pltpu.CompilerParams(vmem_limit_bytes=limit * 1024 * 1024),
        cost_estimate=pl.CostEstimate(flops=flops, bytes_accessed=nbytes, transcendentals=0),
    )(*args)


GELU_C = 0.7978845608028654
GELU_A = 0.044715


def attn_probs_of(query, key):
    scores = dot(query, key, 1, 1) * (HD**-0.5)
    scores = scores - jnp.max(scores, axis=-1, keepdims=True)
    powers = jnp.exp(scores)
    return powers / jnp.sum(powers, axis=-1, keepdims=True)


def forward_kernel(qkv_ref, pre_ref, act_ref):
    probs = attn_probs_of(qkv_ref[:, 0:HD], qkv_ref[:, HD : 2 * HD])
    attended = dot(probs.astype(BF), qkv_ref[:, 2 * HD : 3 * HD], 1, 0)
    act_ref[:, 0:HD] = attended.astype(BF)
    pre = pre_ref[...].astype(F32)
    inner = jnp.tanh(GELU_C * (pre + GELU_A * pre * pre * pre))
    act_ref[:, HD:] = (0.5 * pre * (1.0 + inner)).astype(BF)


def part_of(offset, all_ref, w_attn_ref, w_mlp_ref, part):
    start = pl.multiple_of(image_of(offset) * PATCH, PATCH)
    rows = all_ref[pl.ds(start, PATCH), :]
    part[:, 0:HD] = dot(rows, w_attn_ref[...], 1, 1).astype(BF)
    part[:, HD:] = dot(rows, w_mlp_ref[...], 1, 1).astype(BF)


FIRST = [4, 7, 6, 1]
SECOND = [5, 2, 3, 0]


def spread_kernel(*refs):
    pieces, (w_attn_ref, w_mlp_ref, all_ref), parts = refs[:6], refs[6:9], refs[9:]
    own_pair, other_pair, mine, last, theirs, theirs_last = pieces
    h, z, c = mp_place()
    step = 1 - 2 * c

    def put(piece, place_z, core):
        for dh in range(NH):
            spot = ((h + dh) % NH * NZ + (place_z + 2 * NZ) % NZ) * NC + core
            all_ref[pl.ds(pl.multiple_of(spot * ROWS, ROWS), ROWS), :] = piece[dh]

    put(own_pair, z, c)
    put(other_pair, z, 1 - c)
    for r in range(1, 4):
        put(mine.at[r - 1], z - step * r, c)
        put(theirs.at[r - 1], z + step * r, 1 - c)
    for r in range(1, 3):
        put(mine.at[r + 2], z - step * r, 1 - c)
        put(theirs.at[r + 2], z + step * r, c)
    put(last.at[0], z - step * 4, c)
    put(theirs_last.at[0], z + step * 4, 1 - c)
    put(last.at[1], z - step * 3, 1 - c)
    put(theirs_last.at[1], z + step * 3, c)
    for index, part in zip(FIRST, parts):
        part_of(OFFSETS[index], all_ref, w_attn_ref, w_mlp_ref, part)


def parts_kernel(all_ref, w_attn_ref, w_mlp_ref, *parts):
    for index, part in zip(SECOND, parts):
        part_of(OFFSETS[index], all_ref, w_attn_ref, w_mlp_ref, part)


def middle_kernel(qkv_ref, pre_ref, a_ref, b_ref, c_ref, d_ref, grad_ref):
    total = (
        a_ref[...].astype(F32)
        + b_ref[...].astype(F32)
        + c_ref[...].astype(F32)
        + d_ref[...].astype(F32)
    )
    upward = total[:, 0:HD].astype(BF)
    query, key, value = (qkv_ref[:, i * HD : (i + 1) * HD] for i in range(3))
    probs = attn_probs_of(query, key)
    rounded = probs.astype(BF)
    grad_value = dot(rounded, upward, 0, 0)
    grad_probs = dot(upward, value, 1, 1)
    centred = grad_probs - jnp.sum(grad_probs * probs, axis=-1, keepdims=True)
    grad_scores = (probs * centred * (HD**-0.5)).astype(BF)
    grad_ref[:, 0:HD] = dot(grad_scores, key, 1, 0).astype(BF)
    grad_ref[:, HD : 2 * HD] = dot(grad_scores, query, 0, 0).astype(BF)
    grad_ref[:, 2 * HD : 3 * HD] = grad_value.astype(BF)
    pre = pre_ref[...].astype(F32)
    inner = jnp.tanh(GELU_C * (pre + GELU_A * pre * pre * pre))
    slope = 0.5 * (1.0 + inner) + 0.5 * pre * (1.0 - inner * inner) * (
        GELU_C * (1.0 + 3.0 * GELU_A * pre * pre)
    )
    grad_ref[:, 3 * HD :] = (total[:, HD:] * slope).astype(BF)


def sort_rows(take, offsets, mine_ref, other_ref, rows_ref, sem):
    h, z, c = mp_place()
    step = 1 - 2 * c
    w_qkv_ref, w_mlp_ref = take(0), take(1)
    moves = []
    for k, offset in enumerate(offsets):
        grad = take(k + 2)
        image = image_of(offset)
        rows = dot(grad[:, 0 : 3 * HD], w_qkv_ref[...], 1, 1) + dot(
            grad[:, 3 * HD :], w_mlp_ref[...], 1, 1
        )
        rows_ref[k] = rows.astype(BF)
        dh = (image // 4 + h) % NH
        for half in range(2):
            ahead = ((image % 4 * 2 + half - z) * step + NZ) % NZ
            same = jnp.where(ahead <= 4, ahead, 20 - ahead)
            cross = jnp.where(ahead == 0, 8, jnp.where(ahead <= 3, 4 + ahead, 16 - ahead))
            for core in range(2):
                spot = jnp.where(c == core, same, cross)
                index = half * 2 + core
                source = rows_ref.at[k, pl.ds(index * ROWS, ROWS)]
                moves.append((spot, dh, source, sem.at[k, index]))
                move(moves[-1], mine_ref, other_ref, True)
    return moves


def move(one, mine_ref, other_ref, start):
    spot, dh, source, sem = one

    @pl.when(spot < 8)
    def _():
        copy = pltpu.make_async_copy(source, mine_ref.at[spot, dh], sem)
        copy.start() if start else copy.wait()

    @pl.when(spot >= 8)
    def _():
        copy = pltpu.make_async_copy(source, other_ref.at[spot - 8, dh], sem)
        copy.start() if start else copy.wait()


def early_kernel(take, outs, own):
    mine_ref, other_ref, acc_ref = outs
    moves = sort_rows(take, OFFSETS[:4], mine_ref, other_ref, *own)
    in_part(take, OFFSETS[:4], None, acc_ref)
    for one in moves:
        move(one, mine_ref, other_ref, False)


def late_kernel(take, outs, own):
    mine_ref, other_ref, qkv_ref, mlp_ref, gain_ref = outs
    acc_ref = own[2]
    moves = sort_rows(take, OFFSETS[4:], mine_ref, other_ref, *own[:2])
    in_part(take, OFFSETS[4:], take(7), acc_ref)
    qkv = acc_ref[:, 0 : 3 * HD]
    mlp = acc_ref[:, 3 * HD :]
    qkv_ref[...] = qkv.astype(BF)
    mlp_ref[...] = mlp.astype(BF)
    total = 0.0
    for product in (qkv * take(0)[...].astype(F32), mlp * take(1)[...].astype(F32)):
        for at in range(0, product.shape[1], 128):
            total = total + product[:, at : at + 128]
    total = jnp.broadcast_to(jnp.sum(total.T, axis=0, keepdims=True), gain_ref.shape)
    gain_ref[...] = total
    for one in moves:
        move(one, mine_ref, other_ref, False)


def out_weights_kernel(*refs):
    acts, (all_ref, attn_ref, mlp_ref, acc_ref, act_buffer, row_buffer, sem) = refs[:8], refs[8:]
    copies = []
    for k, offset in enumerate(OFFSETS):
        start = pl.multiple_of(image_of(offset) * PATCH, PATCH)
        copies.append(pltpu.make_async_copy(acts[k], act_buffer.at[k], sem.at[0, k]))
        copies.append(
            pltpu.make_async_copy(all_ref.at[pl.ds(start, PATCH)], row_buffer.at[k], sem.at[1, k])
        )
    for copy in copies:
        copy.start()
    for k in range(8):
        copies[2 * k].wait()
        copies[2 * k + 1].wait()
        term = dot(act_buffer[k], row_buffer[k], 0, 0)
        if k == 0:
            acc_ref[...] = term
        else:
            acc_ref[...] += term
    attn_ref[...] = acc_ref[0:HD].astype(BF)
    mlp_ref[...] = acc_ref[HD:].astype(BF)


def in_part(take, offsets, first, acc_ref):
    all_ref = take(6)
    for k, offset in enumerate(offsets):
        start = pl.multiple_of(image_of(offset) * PATCH, PATCH)
        term = dot(all_ref[pl.ds(start, PATCH), :], take(k + 2)[...], 0, 0)
        before = first if k == 0 else acc_ref
        acc_ref[...] = term if before is None else before[...] + term


def add(*terms):
    total = terms[0].astype(F32)
    for term in terms[1:]:
        total = total + term.astype(F32)
    return total.astype(BF)


def gather_dp_first(own):
    return dp_send(own, Y_UP), dp_send(own, Y_DOWN), dp_send(own, X_SWAP)


def gather_dp_second(below, above, beside):
    return dp_send(beside, Y_DOWN), dp_send(beside, Y_UP)


def gather_dp_third(own, below, above, beside, beside_above, beside_below):
    far = dp_send(below, Y_UP)
    beside_far = dp_send(beside_above, Y_DOWN)
    return [own, above, below, beside, far, beside_above, beside_below, beside_far]


def scatter_dp(parts):
    own, above, below, beside, far, beside_above, beside_below, beside_far = parts
    down = dp_send(far, Y_DOWN)
    up = dp_send(beside_far, Y_UP)
    down_beside = dp_send(beside_below, Y_DOWN)
    up_beside = dp_send(add(beside_above, up), Y_UP)
    down_last = dp_send(add(below, down), Y_DOWN)
    up_last = dp_send(above, Y_UP)
    across = dp_send(add(beside, down_beside, up_beside), X_SWAP)
    return own, down_last, up_last, across


def join_stats(mean, square, count, theirs):
    means = [mean] + [one[0] for one in theirs]
    squares = [square] + [one[1] for one in theirs]
    joined = sum(means) / len(means)
    spread = sum(jnp.square(one - joined) for one in means)
    return joined, sum(squares) + count * spread


def gather_mp(own, act, widened):
    width = widened.shape[1]
    mean = jnp.mean(widened, axis=1)
    square = jnp.sum(jnp.square(widened - mean[:, None]), axis=1)
    theirs = dp_send(jnp.stack([mean, square]), X_SWAP)
    own_pair = jnp.stack([own, mp_send(own, H_SWAP)])
    own_pair, theirs, act = lax.optimization_barrier((own_pair, theirs, act))
    mean, square = join_stats(mean, square, width, [theirs])
    stats = jnp.stack([mean, square])
    theirs = [dp_send(stats, perm) for perm in (Y_UP, Y_DOWN, Y_TWO)]
    other_pair = mp_send(own_pair, C_SWAP)
    mine_a = [mp_send(own_pair, Z_RING)]
    theirs, act = lax.optimization_barrier((theirs, act))
    stats = join_stats(mean, square, 2 * width, theirs)
    first = gather_dp_first(act)
    mine_b = [mp_send(other_pair, Z_RING)]
    mine_a.append(mp_send(mine_a[-1], Z_RING))
    mine_a.append(mp_send(mine_a[-1], Z_RING))
    mine_b.append(mp_send(mine_b[-1], Z_RING))
    mine_a, mine_b, first = lax.optimization_barrier((mine_a, mine_b, first))
    second = gather_dp_second(*first)
    mine = jnp.stack(mine_a + mine_b)
    last = jnp.stack([mp_send(mine_a[-1], Z_RING), mp_send(mine_b[-1], Z_RING)])
    theirs = mp_send(mine, C_SWAP)
    last, theirs, second = lax.optimization_barrier((last, theirs, second))
    theirs_last = mp_send(last, C_SWAP)
    pieces = [own_pair, other_pair, mine, last, theirs, theirs_last]
    return pieces, gather_dp_third(act, *first, *second), stats


def pack(value):
    high = lax.reduce_precision(value, 8, 7)
    middle = lax.reduce_precision(value - high, 8, 7)
    rows = jnp.stack([high, middle, value - high - middle]).astype(BF)
    return jnp.pad(rows, ((0, 13), (0, 0)))


def unpack(rows):
    rows = rows.astype(F32)
    return rows[0] + rows[1] + rows[2]


def with_rows(block, *rows):
    return jnp.concatenate([block.reshape(-1, block.shape[-1]), *rows])


def scatter_mp(mine, other, gain, acts, finish):
    height = 2 * ROWS
    received = mp_send(other, C_SWAP)
    gain = gain + mp_send(gain, C_SWAP)
    received, gain = lax.optimization_barrier((received, gain))
    held = add(mine, received)
    got = mp_send(with_rows(held[4], pack(gain)), Z_RING)
    ring_b = mp_send(held[7], Z_RING)
    passed = []
    for step in range(3):
        rows = got[height:]
        passed.append(rows)
        block = add(held[3 - step].reshape(height, -1), got[:height])
        got = mp_send(with_rows(block, rows), Z_RING)
        if step < 2:
            ring_b = mp_send(add(held[6 - step], ring_b), Z_RING)
            if step == 1:
                got, acts = lax.optimization_barrier((got, acts))
        else:
            ring_b = mp_send(with_rows(ring_b, *passed), C_SWAP)
    ring_a = got[:height].reshape(NH, ROWS, -1)
    opposite = ring_b[height:]
    ring_b = ring_b[:height].reshape(NH, ROWS, -1)
    _, z, c = mp_place()
    step = 1 - 2 * c
    sums = [(z, gain), (z + 4, unpack(got[height:]))]
    for r in range(3):
        sums.append((z - step * (r + 1), unpack(passed[r])))
        sums.append((z + step * (r + 1), unpack(opposite[16 * r : 16 * r + 16])))
    spots = jnp.arange(NZ)[:, None]
    ordered = sum(jnp.where(spots == (at + NZ) % NZ, one[None, :], 0.0) for at, one in sums)
    gain = ordered[0]
    for index in range(1, NZ):
        gain = gain + ordered[index]
    across = mp_send(
        with_rows(add(held[0, 1], ring_a[1], ring_b[1]), pack(gain)), H_SWAP
    )
    across, tied = lax.optimization_barrier((across, finish(acts)))
    total = across[:ROWS].astype(F32)
    for term in (held[0, 0], ring_a[0], ring_b[0]):
        total = total + term.astype(F32)
    gain = unpack(pack(gain)) + unpack(across[ROWS:])
    return total, tied, gain


def sum_dp(values):
    values = values + dp_send(values, X_SWAP)
    others = [dp_send(values, perm) for perm in (Y_UP, Y_DOWN, Y_TWO)]
    return values + others[0] + others[1] + others[2]


def per_device(
    block_input, ln_gain, qkv_act, mlp_pre, out_grad, w_qkv, w_mlp, w_out_attn, w_out_mlp
):
    shape = jax.ShapeDtypeStruct
    widened = block_input.astype(F32)
    act = call(
        forward_kernel, shape((PATCH, 896), BF), 2, 10, flops=10**8, nbytes=2 * 10**6
    )(qkv_act, mlp_pre)
    pieces, all_acts, (mean, square) = gather_mp(out_grad, act, widened)
    inverse = lax.rsqrt(square / D + eps)
    normed = (widened - mean[:, None]) * inverse[:, None]
    scaled = (normed * ln_gain[None, :]).astype(BF)
    all_scaled = lax.all_gather(scaled, "mp", axis=0, tiled=True)
    part_shape = [shape((PATCH, 896), BF)] * 4
    all_grad, *first = call(
        spread_kernel,
        [shape((2048, 768), BF)] + part_shape,
        8,
        16,
        flops=2048 * 768 * 896,
        nbytes=10 * 10**6,
    )(*pieces, w_out_attn, w_out_mlp)
    second = call(parts_kernel, part_shape, 3, 14, flops=2048 * 768 * 896, nbytes=6 * 10**6)(
        all_grad, w_out_attn, w_out_mlp
    )
    parts = [None] * 8
    for index, part in zip(FIRST + SECOND, first + list(second)):
        parts[index] = part
    sums = scatter_dp(parts)
    grad = call(
        middle_kernel, shape((PATCH, 1152), BF), 6, 14, flops=2 * 10**8, nbytes=3 * 10**6
    )(qkv_act, mlp_pre, *sums)
    near = gather_dp_first(grad)
    near, all_scaled = lax.optimization_barrier((near, all_scaled))
    grads = gather_dp_third(grad, *near, *gather_dp_second(*near))
    early, late = grads[:4], grads[4:]
    slots = [shape((8, NH, ROWS, 768), BF)] * 2
    sort_scratch = [pltpu.VMEM((4, PATCH, 768), BF), pltpu.SemaphoreType.DMA((4, 4))]
    mine, other, acc_half = staged_call(
        early_kernel,
        [*slots, shape((768, 1152), F32)],
        [w_qkv, w_mlp, *early, all_scaled],
        24,
        2 * 2048 * 768 * 1152,
        12 * 10**6,
        scratch=sort_scratch,
        any_out=2,
        staged=False,
    )
    late, mine = lax.optimization_barrier((late, mine))
    mine, other, acc_qkv, acc_pre, gain_part = staged_call(
        late_kernel,
        [*slots, shape((768, 384), BF), shape((768, 768), BF), shape((8, 768), F32)],
        [mine, other, w_qkv, w_mlp, *late, all_scaled, acc_half],
        30,
        2 * 2048 * 768 * 1152,
        16 * 10**6,
        scratch=[*sort_scratch, pltpu.VMEM((768, 1152), F32)],
        held=2,
        any_out=2,
        staged=False,
    )

    def finish(acts):
        return pl.pallas_call(
            out_weights_kernel,
            out_shape=[shape((HD, 768), BF), shape((768, 768), BF)],
            in_specs=[pl.BlockSpec(memory_space=pl.ANY)] * 9,
            out_specs=[pl.BlockSpec(memory_space=pltpu.VMEM)] * 2,
            scratch_shapes=[
                pltpu.VMEM((896, 768), F32),
                pltpu.VMEM((8, PATCH, 896), BF),
                pltpu.VMEM((8, PATCH, 768), BF),
                pltpu.SemaphoreType.DMA((2, 8)),
            ],
            compiler_params=pltpu.CompilerParams(vmem_limit_bytes=60 * 1024 * 1024),
            cost_estimate=pl.CostEstimate(
                flops=2 * 2048 * 768 * 896, bytes_accessed=8 * 10**6, transcendentals=0
            ),
        )(*acts, all_grad)

    grad_normed, (acc_attn, acc_mlp), gain_grad = scatter_mp(
        mine, other, gain_part[0] / ln_gain, all_acts, finish
    )
    weighted = grad_normed * ln_gain[None, :]
    sums = jnp.stack([jnp.sum(weighted, axis=1), jnp.sum(weighted * normed, axis=1)])
    sums = sum_dp(sums) / D
    input_grad = out_grad.astype(F32) + inverse[:, None] * (
        weighted - sums[0][:, None] - normed * sums[1][:, None]
    )
    return (input_grad.astype(BF), acc_qkv, acc_pre, acc_attn, acc_mlp, gain_grad)


def solution(mesh):
    return jax.shard_map(
        per_device,
        mesh=mesh,
        in_specs=(
            P("mp", "dp"),
            P("dp"),
            P("dp", "mp"),
            P("dp", "mp"),
            P("mp", "dp"),
            P("dp", "mp"),
            P("dp", "mp"),
            P("mp", "dp"),
            P("mp", "dp"),
        ),
        out_specs=(
            P("mp", "dp"),
            P("dp", "mp"),
            P("dp", "mp"),
            P("mp", "dp"),
            P("mp", "dp"),
            P("dp"),
        ),
        check_vma=False,
    )
```
